256 devices in a mesh: ctx: 128 (over y_lo, x, z, core), dp: 2 (over y_hi).
Axes of the slice: x: 4, y: 4 (y_hi: 2, y_lo: 2; y = y_hi * 2 + y_lo), z: 8, core: 2. Of those that a mesh axis runs over, the one named last changes fastest.
Arguments:
- query_rows: bfloat16 [2, 16384, 4096], P('dp', 'ctx'), may hold values from -6 to 6
- key_rows: bfloat16 [2, 16384, 4096], P('dp', 'ctx'), may hold values from -6 to 6
- value_rows: bfloat16 [2, 16384, 4096], P('dp', 'ctx'), may hold values from -6 to 6
- conv_rows: bfloat16 [2, 16384, 4096], P('dp', 'ctx'), may hold values from -6 to 6
- grad_rows: bfloat16 [2, 16384, 4096], P('dp', 'ctx'), may hold values from -6 to 6
- residues: float32 [4096, 16], replicated, may hold values from -1.5 to 1.5
- decay_rates: float32 [4096, 16], replicated, may hold values from 1.5258789e-05 to 0.125
Outputs:
- grad_query: bfloat16 [2, 16384, 4096], P('dp', 'ctx')
- grad_key: bfloat16 [2, 16384, 4096], P('dp', 'ctx')
- grad_value: bfloat16 [2, 16384, 4096], P('dp', 'ctx')
- grad_coef: float32 [4096, 16], P('ctx')
The draws below stay inside these ranges and needn't reach their ends.
All inputs are finite; a program needn't handle non-finite values.
Results may differ from the reference program's by a relative error of at most 0.012.
Values may be sent and summed in bfloat16 or wider, within the bound.
No kernel may reach another device: no remote copies, remote signals or barrier semaphores. Data moves between devices by JAX's collectives and lax.ppermute only.
A program may use at most 256 MiB of HBM per device.

```python
import math
import jax
import jax.numpy as jnp
from jax import lax

C = 4096
M = 16
LENGTH = 16384
SEQS = 2


def draw_decay_rates(key, part):
    key = jax.random.fold_in(key, 7)
    wide_key = jax.random.fold_in(key, 2)
    lowest = math.log(0.25 / LENGTH)
    highest = math.log(0.125)
    chosen = jnp.exp(jax.random.uniform(wide_key, (C, M), jnp.float32, lowest, highest))
    return chosen.astype(jnp.float32)


def block_scale(rng, shape, cuts, smallest, high):
    def one(dim, blocks):
        heights = jax.random.uniform(jax.random.fold_in(jax.random.fold_in(rng, 6), dim), (blocks,), jnp.float32, smallest / len(cuts), high / len(cuts))
        return jnp.repeat(jnp.exp(heights), shape[dim] // blocks).reshape((-1,) + (1,) * (len(shape) - dim - 1))

    gain = one(*cuts[0])
    for cut in cuts[1:]:
        gain = gain * one(*cut)
    return gain


def centred(own_key, dims, spread, reach, cuts=(), dtype=jnp.bfloat16):
    drawn = spread * jax.random.normal(own_key, dims, jnp.float32)
    if cuts:
        drawn = drawn * block_scale(own_key, dims, cuts, -0.22, 0.18)
    return jnp.clip(drawn, -reach, reach).astype(dtype)


def setup_inputs(seed: int = 0) -> dict:
    seeds = jax.random.split(jax.random.key(seed), 8)
    query_rows = centred(seeds[0], (SEQS, LENGTH, C), 1.0, 6.0, ((0, 2), (1, 128)))
    key_rows = centred(seeds[1], (SEQS, LENGTH, C), 1.0, 6.0, ((0, 2), (1, 128)))
    value_rows = centred(seeds[2], (SEQS, LENGTH, C), 1.0, 6.0, ((0, 2), (1, 128)))
    conv_rows = centred(seeds[3], (SEQS, LENGTH, C), 1.0, 6.0, ((0, 2), (1, 128)))
    grad_rows = centred(seeds[4], (SEQS, LENGTH, C), 1.0, 6.0, ((0, 2), (1, 128)))
    residues = centred(seeds[5], (C, M), M ** -0.5, 1.5, (), jnp.float32)
    decay_rates = draw_decay_rates(jax.random.fold_in(seeds[7], 71), 0)
    return {"query_rows": query_rows, "key_rows": key_rows, "value_rows": value_rows, "conv_rows": conv_rows, "grad_rows": grad_rows, "residues": residues, "decay_rates": decay_rates}


def slab_grads(pieces):
    mixed_slab, product_slab, rate_slab, weight_slab = pieces
    length = mixed_slab.shape[1]
    padded = 2 * length
    positions = jnp.arange(length).astype(jnp.float32)
    powers = jnp.exp(-rate_slab[None, :, :] * positions[:, None, None])
    filter_taps = jnp.einsum('lcm,cm->lc', powers, weight_slab, precision=lax.Precision.HIGHEST)
    taps_hat = jnp.fft.rfft(filter_taps, n=padded, axis=0)
    mixed_hat = jnp.fft.rfft(mixed_slab, n=padded, axis=1)
    product_hat = jnp.fft.rfft(product_slab, n=padded, axis=1)
    grad_mix = jnp.fft.irfft(mixed_hat * jnp.conj(taps_hat)[None], n=padded, axis=1)[:, :length]
    lag_all = jnp.fft.irfft(mixed_hat * jnp.conj(product_hat), n=padded, axis=1)[:, :length]
    lag_grad = lax.optimization_barrier(jnp.sum(lag_all, axis=0))
    coef_sums = jnp.einsum('lc,lcm->cm', lag_grad, powers, precision=lax.Precision.HIGHEST)
    return (grad_mix.astype(jnp.float32), coef_sums)

def reference(query_rows, key_rows, value_rows, conv_rows, grad_rows, residues, decay_rates):
    grad_float = grad_rows.astype(jnp.float32)
    mixed_grad = (grad_float * query_rows.astype(jnp.float32)).astype(jnp.bfloat16)
    product = (key_rows.astype(jnp.float32) * value_rows.astype(jnp.float32)).astype(jnp.bfloat16)
    grad_query = (grad_float * conv_rows.astype(jnp.float32)).astype(jnp.bfloat16)
    gain_table = jnp.sqrt(-jnp.expm1(-2.0 * decay_rates))
    weights = residues * gain_table
    seq_count, length, channels = query_rows.shape
    slab_width = math.gcd(channels, 128)
    groups = channels // slab_width

    def to_slabs(array):
        return array.astype(jnp.float32).reshape(seq_count, length, groups, slab_width).transpose(2, 0, 1, 3)
    grad_mix, coef_sums = lax.map(slab_grads, (to_slabs(mixed_grad), to_slabs(product), decay_rates.reshape(groups, slab_width, -1), weights.reshape(groups, slab_width, -1)))
    grad_mix = grad_mix.transpose(1, 2, 0, 3).reshape(seq_count, length, channels).astype(jnp.bfloat16)
    grad_coef = gain_table * coef_sums.reshape(channels, -1) / math.sqrt(length)
    mix_float = grad_mix.astype(jnp.float32)
    grad_key = (mix_float * value_rows.astype(jnp.float32)).astype(jnp.bfloat16)
    grad_value = (mix_float * key_rows.astype(jnp.float32)).astype(jnp.bfloat16)
    return (grad_query, grad_key, grad_value, grad_coef)
```

```python
import functools
import math

import jax
import jax.numpy as jnp
from jax import lax
from jax.experimental import pallas as pl
from jax.experimental.pallas import tpu as pltpu
from jax.sharding import PartitionSpec as P

F32 = jnp.float32
BF16 = jnp.bfloat16
LANES = 128
SUB = 8
TOKENS = 128
ROWS = TOKENS // SUB
MODES = 16
WIDTH = 512
TILES = WIDTH // LANES
VMEM_LIMIT = 48 * 1024 * 1024


def lane_slice(tile):
    return pl.ds(pl.multiple_of(tile * LANES, LANES), LANES)


def transposed(rows):
    count = rows.shape[1]
    first = lax.broadcasted_iota(jnp.int32, (count, count), 0)
    second = lax.broadcasted_iota(jnp.int32, (count, count), 1)
    unit = (first == second).astype(F32)
    return lax.dot_general(
        unit, rows, (((1,), (1,)), ((), ())), precision=lax.Precision.HIGHEST, preferred_element_type=F32
    )


def gain_of(rates):
    square = rates * rates
    series = 1.0 + square * (1.0 / 6.0 + square * (1.0 / 120.0 + square * (1.0 / 5040.0)))
    return jnp.sqrt(2.0 * rates * series * jnp.exp(-rates))


def wide(row):
    return jnp.broadcast_to(row, (SUB, LANES))


def swap_quarters(tile):
    j = lax.broadcasted_iota(jnp.int32, (SUB, LANES), 0) & 3
    q = lax.broadcasted_iota(jnp.int32, (SUB, LANES), 1) >> 5
    for bit in (1, 2):
        j_set = (j & bit) != 0
        q_set = (q & bit) != 0
        up = pltpu.roll(pltpu.roll(tile, bit, 0), LANES - 32 * bit, 1)
        down = pltpu.roll(pltpu.roll(tile, SUB - bit, 0), 32 * bit, 1)
        tile = jnp.where(j_set == q_set, tile, jnp.where(j_set, up, down))
    return tile


def scatter_rows(modes_ref, slab_ref, first):
    for pair in range(2):
        moved = swap_quarters(modes_ref[SUB * pair : SUB * pair + SUB, :])
        for k in range(2):
            for q in range(4):
                row = SUB * q + first + 2 * pair + k
                slab_ref[row : row + 1, :] = moved[4 * k + q : 4 * k + q + 1, :]


def summary_kernel(
    grad_ref, query_ref, key_ref, value_ref, decay_ref,
    mixed_ref, product_ref, rate_ref, send_ref,
    powers, mixed_tile, product_tile, state_rows, carry_rows, slab,
):
    rates = transposed(decay_ref[...])
    rate_ref[...] = rates
    for index, power in enumerate((1.0, 2.0, 4.0, 8.0)):
        powers[index] = jnp.exp(-power * rates)

    def one_tile(tile, _):
        lanes = lane_slice(tile)
        mixed = (grad_ref[:, lanes].astype(F32) * query_ref[:, lanes].astype(F32)).astype(BF16)
        product = (key_ref[:, lanes].astype(F32) * value_ref[:, lanes].astype(F32)).astype(BF16)
        mixed_ref[:, lanes] = mixed
        product_ref[:, lanes] = product
        mixed_tile[...] = mixed.astype(F32)
        product_tile[...] = product.astype(F32)
        for base in range(0, MODES, 4):
            group = range(base, base + 4)
            eighth = [wide(powers[3, m : m + 1, lanes]) for m in group]
            state = [mixed_tile[TOKENS - SUB :, :]] * 4
            carry = [product_tile[:SUB, :]] * 4
            for i in range(1, ROWS):
                low = TOKENS - SUB - SUB * i
                mixed_row = mixed_tile[low : low + SUB, :]
                product_row = product_tile[SUB * i : SUB * i + SUB, :]
                state = [s * a + mixed_row for s, a in zip(state, eighth)]
                carry = [c * a + product_row for c, a in zip(carry, eighth)]
            for at, m in enumerate(group):
                one, two, four = [wide(powers[p, m : m + 1, lanes]) for p in range(3)]
                s = state[at]
                s = s + four * pltpu.roll(s, 4, 0)
                s = s + two * pltpu.roll(s, 6, 0)
                s = s + one * pltpu.roll(s, 7, 0)
                state_rows[m : m + 1, :] = s[0:1, :]
                c = carry[at]
                c = c + one * pltpu.roll(c, 1, 0)
                c = c + two * pltpu.roll(c, 2, 0)
                c = (c + four * pltpu.roll(c, 4, 0)) * one
                carry_rows[m : m + 1, :] = c[7:8, :]
        scatter_rows(state_rows, slab, 0)
        scatter_rows(carry_rows, slab, 4)
        send_ref[pl.ds(pl.multiple_of(tile * 32, 32), 32), :] = slab[...].astype(BF16)
        return 0

    lax.fori_loop(0, TILES, one_tile, 0)


def local_kernel(
    mixed_ref, product_ref, rate_ref, residue_ref,
    near_ref, send_ref,
    powers, weights, mixed_tile, product_tile, near_tile, coef_rows, slab,
):
    rates = rate_ref[...]
    weights[...] = transposed(residue_ref[...]) * gain_of(rates)
    for index, power in enumerate((1.0, 16.0, 32.0, 64.0)):
        powers[index] = jnp.exp(-power * rates)
    place = lax.broadcasted_iota(jnp.int32, (SUB, LANES), 0)
    slab[...] = jnp.zeros_like(slab)

    def one_tile(tile, _):
        lanes = lane_slice(tile)
        mixed_tile[...] = mixed_ref[:, lanes].astype(F32)
        product_tile[...] = product_ref[:, lanes].astype(F32)
        for base in range(0, MODES, 8):
            group = range(base, base + 8)
            one = [wide(powers[0, m : m + 1, lanes]) for m in group]
            weight = [wide(weights[m : m + 1, lanes]) for m in group]
            state = [mixed_tile[pl.ds(ROWS - 1, SUB, stride=ROWS), :]] * 8
            for j in range(ROWS - 2, -1, -1):
                mixed_row = mixed_tile[pl.ds(j, SUB, stride=ROWS), :]
                state = [s * a + mixed_row for s, a in zip(state, one)]
            for at, m in enumerate(group):
                s = state[at]
                for index, step in ((1, 1), (2, 2), (3, 4)):
                    shifted = jnp.where(place < SUB - step, pltpu.roll(s, SUB - step, 0), 0.0)
                    s = s + wide(powers[index, m : m + 1, lanes]) * shifted
                state[at] = jnp.where(place < SUB - 1, pltpu.roll(s, SUB - 1, 0), 0.0)
            total = [None] * 8
            for j in range(ROWS - 1, -1, -1):
                mixed_row = mixed_tile[pl.ds(j, SUB, stride=ROWS), :]
                product_row = product_tile[pl.ds(j, SUB, stride=ROWS), :]
                state = [s * a + mixed_row for s, a in zip(state, one)]
                terms = [s * w for s, w in zip(state, weight)]
                while len(terms) > 1:
                    terms = [x + y for x, y in zip(terms[::2], terms[1::2])]
                rows = slice(SUB * j, SUB * j + SUB)
                near_tile[rows, :] = terms[0] if base == 0 else near_tile[rows, :] + terms[0]
                total = [s * product_row if t is None else t + s * product_row for s, t in zip(state, total)]
            for at, m in enumerate(group):
                t = total[at]
                t = t + pltpu.roll(t, 4, 0)
                t = t + pltpu.roll(t, 2, 0)
                t = t + pltpu.roll(t, 1, 0)
                coef_rows[m : m + 1, :] = t[0:1, :]
        for i in range(ROWS):
            near_ref[SUB * i : SUB * i + SUB, lanes] = near_tile[pl.ds(64 * (i % 2) + i // 2, SUB, stride=SUB), :]
        scatter_rows(coef_rows, slab, 4)
        send_ref[pl.ds(pl.multiple_of(tile * 32, 32), 32), :] = slab[...].astype(BF16)
        return 0

    lax.fori_loop(0, TILES, one_tile, 0)


def scan_kernel(blocks, received_ref, coef_ref, rate_ref, send_ref, far_ref):
    decay = jnp.exp(-float(TOKENS) * rate_ref[...])
    low = lax.broadcasted_iota(jnp.int32, (SUB, LANES), 0) < 4

    def step(back, held):
        state, far = held
        start = pl.multiple_of((blocks // 2 - 1 - back) * 16, 16)
        pair = received_ref[pl.ds(start, 16), :].astype(F32)
        coef = coef_ref[pl.ds(start, 16), :].astype(F32)
        out = [None, None]
        for which in (1, 0):
            here = pair[SUB * which : SUB * which + SUB, :]
            out[which] = jnp.where(low, state, coef[SUB * which : SUB * which + SUB, :])
            far = far + here * state
            state = jnp.where(low, here, pltpu.roll(here, 4, 0)) + decay * state
        send_ref[pl.ds(start, 16), :] = jnp.concatenate(out, axis=0).astype(BF16)
        return state, far

    zero = jnp.zeros((SUB, LANES), F32)
    _, far = lax.fori_loop(0, blocks // 2, step, (zero, zero), unroll=4)
    far_ref[...] = far


def coef_kernel(blocks, scale, received_ref, far_ref, rate_ref, out_ref):
    def step(at, held):
        rows = received_ref[pl.ds(pl.multiple_of(at * 16, 16), 16), :].astype(F32)
        return held[0] + rows[:SUB, :], held[1] + rows[SUB:, :]

    first, second = lax.fori_loop(0, blocks // 2, step, (far_ref[...], jnp.zeros((SUB, LANES), F32)), unroll=8)
    out_ref[...] = (first + second) * gain_of(rate_ref[...]) * scale


def output_kernel(
    near_ref, received_ref, rate_ref, residue_ref, key_ref, value_ref,
    grad_key_ref, grad_value_ref,
    powers, weights, slab, heads,
):
    rates = rate_ref[...]
    weights[...] = transposed(residue_ref[...]) * gain_of(rates)
    powers[...] = jnp.exp(-8.0 * rates)
    back = (SUB - lax.broadcasted_iota(jnp.int32, (SUB, LANES), 0)).astype(F32)

    def one_tile(tile, _):
        lanes = lane_slice(tile)
        slab[...] = received_ref[pl.ds(pl.multiple_of(tile * 32, 32), 32), :].astype(F32)
        for pair in range(2):
            parts = [slab[pl.ds(2 * pair + k, 4, stride=SUB), :] for k in range(2)]
            heads[SUB * pair : SUB * pair + SUB, :] = swap_quarters(jnp.concatenate(parts, axis=0))
        heads[...] = heads[...] * weights[:, lanes]
        eighth = [wide(powers[m : m + 1, lanes]) for m in range(MODES)]
        state = [
            wide(heads[m : m + 1, :]) * jnp.exp(-back * wide(rate_ref[m : m + 1, lanes])) for m in range(MODES)
        ]
        for i in range(ROWS - 1, -1, -2):
            both = []
            for row in (i, i - 1):
                terms = state
                while len(terms) > 1:
                    terms = [x + y for x, y in zip(terms[::2], terms[1::2])]
                both.append(near_ref[SUB * row : SUB * row + SUB, lanes] + terms[0])
                if row > 0:
                    state = [s * a for s, a in zip(state, eighth)]
            rows = slice(SUB * (i - 1), SUB * (i - 1) + 16)
            mix = jnp.concatenate(both[::-1], axis=0).astype(BF16).astype(F32)
            grad_key_ref[rows, lanes] = (mix * value_ref[rows, lanes].astype(F32)).astype(BF16)
            grad_value_ref[rows, lanes] = (mix * key_ref[rows, lanes].astype(F32)).astype(BF16)
        return 0

    lax.fori_loop(0, TILES, one_tile, 0)


def gate_kernel(grad_ref, conv_ref, out_ref):
    out_ref[...] = (grad_ref[...].astype(F32) * conv_ref[...].astype(F32)).astype(BF16)


def call(kernel, grid, in_specs, out_specs, out_shape, scratch, flops, moved):
    return pl.pallas_call(
        kernel,
        grid=grid,
        in_specs=in_specs,
        out_specs=out_specs,
        out_shape=out_shape,
        scratch_shapes=scratch,
        compiler_params=pltpu.CompilerParams(vmem_limit_bytes=VMEM_LIMIT),
        cost_estimate=pl.CostEstimate(flops=flops, bytes_accessed=moved, transcendentals=0),
    )


def local(query_rows, key_rows, value_rows, conv_rows, grad_rows, residues, decay_rates):
    blocks = lax.axis_size("ctx")
    tokens, channels = query_rows.shape[1:]
    steps = channels // WIDTH
    own = channels // blocks
    length = blocks * tokens
    query, key, value, conv, grad = (x[0] for x in (query_rows, key_rows, value_rows, conv_rows, grad_rows))

    token_block = pl.BlockSpec((tokens, WIDTH), lambda n: (0, n))
    table_block = pl.BlockSpec((WIDTH, MODES), lambda n: (n, 0))
    mode_block = pl.BlockSpec((MODES, WIDTH), lambda n: (0, n))
    slab_block = pl.BlockSpec((TILES * 32, LANES), lambda n: (n, 0))
    token_half = jax.ShapeDtypeStruct((tokens, channels), BF16)
    token_full = jax.ShapeDtypeStruct((tokens, channels), F32)
    mode_table = jax.ShapeDtypeStruct((MODES, channels), F32)
    slabs = jax.ShapeDtypeStruct((blocks * SUB, LANES), BF16)
    tile_scratch = pltpu.VMEM((TOKENS, LANES), F32)
    rows_scratch = pltpu.VMEM((MODES, LANES), F32)
    slab_scratch = pltpu.VMEM((32, LANES), F32)

    mixed, product, rates, summary = call(
        summary_kernel, (steps,),
        [token_block] * 4 + [table_block],
        [token_block, token_block, mode_block, slab_block],
        [token_half, token_half, mode_table, slabs],
        [pltpu.VMEM((4, MODES, WIDTH), F32), tile_scratch, tile_scratch, rows_scratch, rows_scratch, slab_scratch],
        10**9, 8 * 2**20,
    )(grad, query, key, value, decay_rates)

    def exchange(rows):
        moved = lax.all_to_all(rows.reshape(blocks, SUB, LANES), "ctx", split_axis=0, concat_axis=0, tiled=True)
        return moved.reshape(blocks * SUB, LANES)

    received = exchange(summary)

    near, coef_slabs = call(
        local_kernel, (steps,),
        [token_block, token_block, mode_block, table_block],
        [token_block, slab_block],
        [token_full, slabs],
        [
            pltpu.VMEM((4, MODES, WIDTH), F32), pltpu.VMEM((MODES, WIDTH), F32),
            tile_scratch, tile_scratch, tile_scratch, rows_scratch, slab_scratch,
        ],
        2 * 10**9, 6 * 2**20,
    )(mixed, product, rates, residues)

    first = lax.axis_index("ctx") * own
    rate_own, _ = lax.optimization_barrier((lax.dynamic_slice_in_dim(decay_rates, first, own, 0), summary))
    rate_own = rate_own.T.reshape(4, LANES)
    rate_own = jnp.concatenate([rate_own, rate_own], axis=0)

    whole = lambda rows, dtype: (pl.BlockSpec((rows, LANES), lambda: (0, 0)), jax.ShapeDtypeStruct((rows, LANES), dtype))
    slab_spec, _ = whole(blocks * SUB, BF16)
    small_spec, small = whole(SUB, F32)
    carries, far = call(
        functools.partial(scan_kernel, blocks), (),
        [slab_spec, slab_spec, small_spec], [slab_spec, small_spec], [slabs, small], [],
        10**6, 2**20,
    )(received, coef_slabs, rate_own)

    returned = exchange(carries)

    gate_in, _ = lax.optimization_barrier((conv, carries))
    grad_query = call(
        gate_kernel, (4,),
        [pl.BlockSpec((tokens, channels // 4), lambda n: (0, n))] * 2,
        pl.BlockSpec((tokens, channels // 4), lambda n: (0, n)), token_half, [],
        10**6, 3 * 2**20,
    )(grad, gate_in)

    coef_part = call(
        functools.partial(coef_kernel, blocks, 1.0 / math.sqrt(length)), (),
        [slab_spec, small_spec, small_spec], small_spec, small, [],
        10**6, 2**18,
    )(returned, far, rate_own)
    other = lax.ppermute(coef_part, "dp", [(0, 1), (1, 0)])

    grad_key, grad_value = call(
        output_kernel, (steps,),
        [token_block, slab_block, mode_block, table_block, token_block, token_block],
        [token_block, token_block], [token_half, token_half],
        [pltpu.VMEM((MODES, WIDTH), F32), pltpu.VMEM((MODES, WIDTH), F32), slab_scratch, rows_scratch],
        10**9, 6 * 2**20,
    )(near, returned, rates, residues, key, value)

    coef = (coef_part + other)[4:].reshape(4, 4, own).transpose(2, 0, 1).reshape(own, MODES)
    return (grad_query[None], grad_key[None], grad_value[None], coef)


def solution(mesh):
    rows = P("dp", "ctx", None)
    return jax.shard_map(
        local,
        mesh=mesh,
        in_specs=(rows, rows, rows, rows, rows, P(), P()),
        out_specs=(rows, rows, rows, P("ctx", None)),
        check_vma=False,
    )
```

```python
import functools
import math

import jax
import jax.numpy as jnp
from jax import lax
from jax.experimental import pallas as pl
from jax.experimental.pallas import tpu as pltpu
from jax.sharding import PartitionSpec as P

F32 = jnp.float32
BF16 = jnp.bfloat16
LANES = 128
SUB = 8
TOKENS = 128
ROWS = TOKENS // SUB
MODES = 16
QUADS = 4
WIDTH = 1024
VMEM_LIMIT = 60 * 1024 * 1024
SMALL_LIMIT = 4 * 1024 * 1024


def lane_slice(tile):
    return pl.ds(pl.multiple_of(tile * LANES, LANES), LANES)


def slab_rows(tile):
    return pl.ds(pl.multiple_of(tile * 32, 32), 32)


def gain_of(rates):
    square = rates * rates
    series = 1.0 + square * (1.0 / 6.0 + square * (1.0 / 120.0 + square * (1.0 / 5040.0)))
    return jnp.sqrt(2.0 * rates * series * jnp.exp(-rates))


def wide(row):
    return jnp.broadcast_to(row, (SUB, LANES))


def halves_sum(terms):
    while len(terms) > 1:
        terms = [x + y for x, y in zip(terms[::2], terms[1::2])]
    return terms[0]


def swap_quarters(tile):
    j = lax.broadcasted_iota(jnp.int32, (SUB, LANES), 0) & 3
    q = lax.broadcasted_iota(jnp.int32, (SUB, LANES), 1) >> 5
    for bit in (1, 2):
        j_set = (j & bit) != 0
        q_set = (q & bit) != 0
        up, down = pltpu.roll(tile, bit, 0), pltpu.roll(tile, SUB - bit, 0)
        if bit == 2:
            moved = pltpu.roll(jnp.where(j_set, up, down), 64, 1)
        else:
            moved = jnp.where(j_set, pltpu.roll(up, LANES - 32, 1), pltpu.roll(down, 32, 1))
        tile = jnp.where(j_set == q_set, tile, moved)
    return tile


def natural(tokens_sub, row):
    return tokens_sub[pl.ds(64 * (row % 2) + row // 2, SUB, stride=SUB), :]


def fold(first, second, bit, place):
    clear = (place & bit) == 0
    left = jnp.where(clear, first, pltpu.roll(second, bit, 0))
    right = jnp.where(clear, pltpu.roll(first, SUB - bit, 0), second)
    return left + right


def sublane_sums(tiles, place):
    for bit in (4, 2, 1):
        tiles = [fold(tiles[i], tiles[i + bit], bit, place) for i in range(bit)]
    return tiles[0]


def each_tile(width, body, slots=2):
    def some(at, _):
        for slot in range(slots):
            body(slots * at + slot, slot)
        return 0

    lax.fori_loop(0, width // (slots * LANES), some, 0)


def weighted_sums(state, entry, rows_of, place):
    for bit, power in ((4, 3), (2, 2), (1, 1)):
        clear = (place & bit) == 0
        weights = [rows_of(power, bit, i) for i in range(bit)]
        for which, tiles in enumerate((state, entry)):
            folded = []
            for i, weight in enumerate(weights):
                first, second = tiles[i], tiles[i + bit]
                left = jnp.where(clear, first, pltpu.roll(second, bit, 0))
                right = jnp.where(clear, pltpu.roll(first, SUB - bit, 0), second)
                folded.append(left + weight * right if which == 0 else right + weight * left)
            if which == 0:
                state = folded
            else:
                entry = folded
    return state[0], entry[0]


def summary_kernel(
    grad_ref, query_ref, key_ref, value_ref, rate_ref,
    mixed_ref, product_ref, state_ref, entry_ref, send_ref,
    powers, full,
):
    rates = rate_ref[...]
    for index, power in enumerate((1.0, 16.0, 32.0, 64.0)):
        powers[index] = jnp.exp(-power * rates)
    place = lax.broadcasted_iota(jnp.int32, (SUB, LANES), 0)

    def body(tile, slot):
        lanes = lane_slice(tile)
        mixed_full, product_full = full.at[slot, 0], full.at[slot, 1]
        mixed = (grad_ref[:, lanes].astype(F32) * query_ref[:, lanes].astype(F32)).astype(BF16)
        product = (key_ref[:, lanes].astype(F32) * value_ref[:, lanes].astype(F32)).astype(BF16)
        mixed_full[...] = mixed.astype(F32)
        product_full[...] = product.astype(F32)
        g = [mixed_full[pl.ds(j, SUB, stride=ROWS), :] for j in range(ROWS)]
        p = [product_full[pl.ds(j, SUB, stride=ROWS), :] for j in range(ROWS)]
        for j in range(0, ROWS, 2):
            rows = slice(SUB * j, SUB * j + 16)
            mixed_ref[rows, lanes] = jnp.concatenate([g[j], g[j + 1]], axis=0).astype(BF16)
            product_ref[rows, lanes] = jnp.concatenate([p[j], p[j + 1]], axis=0).astype(BF16)
        sums = []
        for half in range(2):
            states, entries = [], []
            for base in range(SUB * half, SUB * half + SUB, 4):
                group = range(base, base + 4)
                one = [wide(powers[0, m : m + 1, lanes]) for m in group]
                state = [g[ROWS - 1]] * 4
                entry = [p[0] * a for a in one]
                for i in range(1, ROWS):
                    state = [s * a + g[ROWS - 1 - i] for s, a in zip(state, one)]
                    entry = [(e + p[i]) * a for e, a in zip(entry, one)]
                for s, e, m in zip(state, entry, group):
                    state_ref[SUB * m : SUB * m + SUB, lanes] = s
                    entry_ref[SUB * m : SUB * m + SUB, lanes] = e
                states += state
                entries += entry

            def rows_of(power, bit, i):
                if bit == 1:
                    return powers[power, SUB * half : SUB * half + SUB, lanes]
                modes = [SUB * half + i + bit * at for at in range(SUB // bit)]
                out = wide(powers[power, modes[-1] : modes[-1] + 1, lanes])
                for at in range(len(modes) - 2, -1, -1):
                    out = jnp.where(place < bit * (at + 1), wide(powers[power, modes[at] : modes[at] + 1, lanes]), out)
                return out

            s, e = weighted_sums(states, entries, rows_of, place)
            low = place < 4
            sums += [jnp.where(low, s, pltpu.roll(e, 4, 0)), jnp.where(low, pltpu.roll(s, 4, 0), e)]
        send_ref[slab_rows(tile), :] = jnp.concatenate(sums, axis=0).astype(BF16)

    each_tile(grad_ref.shape[1], body)


def local_kernel(
    scale, mixed_ref, product_ref, state_ref, entry_ref, rate_ref, residue_ref,
    near_ref, lead_ref, send_ref,
    powers, weights, taps, lags, slabs, runs,
):
    rates = rate_ref[...]
    powers[...] = jnp.exp(-rates)
    gains = gain_of(rates)
    term = residue_ref[...] * gains
    for d in range(ROWS):
        taps[d : d + 1, :] = jnp.sum(term, axis=0, keepdims=True)
        term = term * powers[...]
        if d == 0:
            weights[...] = term
    for index, power in enumerate((16.0, 32.0, 64.0)):
        runs[index] = jnp.exp(-power * rates)
    place = lax.broadcasted_iota(jnp.int32, (SUB, LANES), 0)

    def body(tile, slot):
        lanes = lane_slice(tile)
        g, p = [], []
        for j in range(0, ROWS, 2):
            rows = slice(SUB * j, SUB * j + 16)
            pair = mixed_ref[rows, lanes].astype(F32)
            g += [pair[:SUB, :], pair[SUB:, :]]
            pair = product_ref[rows, lanes].astype(F32)
            p += [pair[:SUB, :], pair[SUB:, :]]
        near = [None] * ROWS
        for d in range(ROWS):
            tap = wide(taps[d : d + 1, lanes])
            for j in range(ROWS - d):
                near[j] = tap * g[j + d] if d == 0 else near[j] + tap * g[j + d]
        for j in range(ROWS):
            near_ref[SUB * j : SUB * j + SUB, lanes] = near[j]
        lag = []
        for d in range(ROWS):
            total = g[d] * p[0]
            for j in range(1, ROWS - d):
                total = total + g[j + d] * p[j]
            lag.append(total)
        for half in range(2):
            rows = slice(SUB * half, SUB * half + SUB)
            lags[0, rows, lanes] = sublane_sums(lag[rows], place)
            cross = []
            for m in range(SUB * half, SUB * half + SUB):
                mode_rows = slice(SUB * m, SUB * m + SUB)
                carry = state_ref[mode_rows, lanes]
                for index, step in ((0, 1), (1, 2), (2, 4)):
                    later = jnp.where(place < SUB - step, pltpu.roll(carry, SUB - step, 0), 0.0)
                    carry = carry + wide(runs[index, m : m + 1, lanes]) * later
                carry = jnp.where(place < SUB - 1, pltpu.roll(carry, SUB - 1, 0), 0.0)
                cross.append(carry * entry_ref[mode_rows, lanes])
                lead_ref[mode_rows, lanes] = carry * wide(weights[m : m + 1, lanes])
            lags[1, rows, lanes] = sublane_sums(cross, place)

    each_tile(mixed_ref.shape[1], body)
    coef = jnp.broadcast_to(lags[0, ROWS - 1 : ROWS, :], rates.shape)
    for d in range(ROWS - 2, -1, -1):
        coef = coef * powers[...] + lags[0, d : d + 1, :]
    lags[1] = (coef + lags[1]) * gains * scale
    slabs[...] = jnp.zeros_like(slabs)

    def ship(tile, slot):
        lanes = lane_slice(tile)
        slab = slabs.at[slot]
        for pair in range(2):
            moved = swap_quarters(lags[1, SUB * pair : SUB * pair + SUB, lanes])
            for k in range(2):
                for q in range(4):
                    row = SUB * q + 4 + 2 * pair + k
                    slab[row : row + 1, :] = moved[4 * k + q : 4 * k + q + 1, :]
        send_ref[slab_rows(tile), :] = slab[...].astype(BF16)

    each_tile(mixed_ref.shape[1], ship, 8)


def scan_kernel(scale, received_ref, coef_ref, rate_ref, send_ref):
    blocks = received_ref.shape[0] // SUB
    rates = rate_ref[...]
    decay = jnp.exp(-float(TOKENS) * rates)
    place = lax.broadcasted_iota(jnp.int32, (SUB, LANES), 0)
    low = place < 4

    def step(back, held):
        state, far = held
        start = pl.multiple_of((blocks // 2 - 1 - back) * 16, 16)
        pair = received_ref[pl.ds(start, 16), :].astype(F32)
        coef = coef_ref[pl.ds(start, 16), :].astype(F32)
        out = [None, None]
        for which in (1, 0):
            here = pair[SUB * which : SUB * which + SUB, :]
            out[which] = jnp.where(low, state, coef[SUB * which : SUB * which + SUB, :])
            far = far + here * state
            state = jnp.where(low, here, pltpu.roll(here, 4, 0)) + decay * state
        send_ref[pl.ds(start, 16), :] = jnp.concatenate(out, axis=0).astype(BF16)
        return state, far

    zero = jnp.zeros((SUB, LANES), F32)
    _, far = lax.fori_loop(0, blocks // 2, step, (zero, zero), unroll=4)
    far = swap_quarters(far * gain_of(rates) * scale)
    me = lax.axis_index("ctx")
    mine = slab_rows(me // QUADS)
    extra = [jnp.where(place == 4 + me % QUADS, wide(far[4 + q : 5 + q, :]), 0.0) for q in range(QUADS)]
    send_ref[mine, :] = (send_ref[mine, :].astype(F32) + jnp.concatenate(extra, axis=0)).astype(BF16)


def total_kernel(received_ref, out_ref):
    def step(at, held):
        rows = received_ref[pl.ds(pl.multiple_of(at * 16, 16), 16), :].astype(F32)
        return held[0] + rows[:SUB, :], held[1] + rows[SUB:, :]

    zero = jnp.zeros((SUB, LANES), F32)
    first, second = lax.fori_loop(0, received_ref.shape[0] // 16, step, (zero, zero), unroll=8)
    out_ref[...] = first + second


def output_kernel(
    near_ref, lead_ref, received_ref, rate_ref, residue_ref, key_ref, value_ref,
    grad_key_ref, grad_value_ref,
    powers, weights, slabs, mixes,
):
    rates = rate_ref[...]
    powers[...] = jnp.exp(-rates)
    weights[...] = residue_ref[...] * gain_of(rates) * powers[...]
    back = (16 * (SUB - 1 - lax.broadcasted_iota(jnp.int32, (SUB, LANES), 0))).astype(F32)

    def body(tile, slot):
        lanes = lane_slice(tile)
        slab, mix_sub = slabs.at[slot], mixes.at[slot]
        slab[...] = received_ref[slab_rows(tile), :].astype(F32)
        one = [wide(powers[m : m + 1, lanes]) for m in range(MODES)]
        state = []
        for m in range(MODES):
            row = SUB * (m // 4) + m % 4
            head = wide(slab[row : row + 1, :] * weights[m : m + 1, lanes])
            reach = jnp.exp(-back * wide(rate_ref[m : m + 1, lanes]))
            state.append(lead_ref[SUB * m : SUB * m + SUB, lanes] + head * reach)
        for j in range(ROWS - 1, -1, -1):
            rows = slice(SUB * j, SUB * j + SUB)
            mix_sub[rows, :] = near_ref[rows, lanes] + halves_sum(state)
            if j > 0:
                state = [s * a for s, a in zip(state, one)]
        for i in range(0, ROWS, 2):
            rows = slice(SUB * i, SUB * i + 16)
            mix = jnp.concatenate([natural(mix_sub, i), natural(mix_sub, i + 1)], axis=0).astype(BF16).astype(F32)
            grad_key_ref[rows, lanes] = (mix * value_ref[rows, lanes].astype(F32)).astype(BF16)
            grad_value_ref[rows, lanes] = (mix * key_ref[rows, lanes].astype(F32)).astype(BF16)

    each_tile(near_ref.shape[1], body)


def gate_kernel(grad_ref, conv_ref, out_ref):
    out_ref[...] = (grad_ref[...].astype(F32) * conv_ref[...].astype(F32)).astype(BF16)


def call(kernel, grid, in_specs, out_specs, out_shape, scratch=(), flops=10**6, moved=2**20, limit=VMEM_LIMIT):
    return pl.pallas_call(
        kernel,
        grid=grid,
        in_specs=in_specs,
        out_specs=out_specs,
        out_shape=out_shape,
        scratch_shapes=scratch,
        compiler_params=pltpu.CompilerParams(vmem_limit_bytes=limit),
        cost_estimate=pl.CostEstimate(flops=flops, bytes_accessed=moved, transcendentals=0),
    )


def local(query_rows, key_rows, value_rows, conv_rows, grad_rows, residues, decay_rates):
    blocks = lax.axis_size("ctx")
    tokens, channels = query_rows.shape[1:]
    own = channels // blocks
    scale = 1.0 / math.sqrt(blocks * tokens)
    query, key, value, conv, grad = (x[0] for x in (query_rows, key_rows, value_rows, conv_rows, grad_rows))
    rates, residue = decay_rates.T, residues.T

    def table(*shape):
        return pltpu.VMEM(shape, F32)

    token_block = pl.BlockSpec((tokens, WIDTH), lambda n: (0, n))
    mode_block = pl.BlockSpec((MODES, WIDTH), lambda n: (0, n))
    slab_block = pl.BlockSpec((WIDTH // LANES * 32, LANES), lambda n: (n, 0))
    token_half = jax.ShapeDtypeStruct((tokens, channels), BF16)
    token_full = jax.ShapeDtypeStruct((tokens, channels), F32)
    slabs = jax.ShapeDtypeStruct((blocks * SUB, LANES), BF16)
    steps = (channels // WIDTH,)

    mixed, product, states, entries, summary = call(
        summary_kernel, steps,
        [token_block] * 4 + [mode_block],
        [token_block] * 4 + [slab_block],
        [token_half, token_half, token_full, token_full, slabs],
        [table(4, MODES, WIDTH), table(2, 2, TOKENS, LANES)],
        10**9, 10 * 2**20,
    )(grad, query, key, value, rates)

    def exchange(rows):
        moved = lax.all_to_all(rows.reshape(blocks, SUB, LANES), "ctx", split_axis=0, concat_axis=0, tiled=True)
        return moved.reshape(blocks * SUB, LANES)

    received = exchange(summary)

    near, lead, coef_slabs = call(
        functools.partial(local_kernel, scale), steps,
        [token_block] * 4 + [mode_block] * 2,
        [token_block, token_block, slab_block],
        [token_full, token_full, slabs],
        [
            table(MODES, WIDTH), table(MODES, WIDTH), table(MODES, WIDTH), table(2, MODES, WIDTH),
            table(8, 32, LANES), table(3, MODES, WIDTH),
        ],
        10**9, 10 * 2**20,
    )(mixed, product, states, entries, rates, residue)

    me = lax.axis_index("ctx")
    rates_late, _ = lax.optimization_barrier((rates, summary))
    rate_own = lax.dynamic_slice(rates_late, (4 * (me % QUADS), LANES * (me // QUADS)), (4, LANES))
    rate_own = jnp.concatenate([rate_own, rate_own], axis=0)

    vmem = pl.BlockSpec(memory_space=pltpu.VMEM)
    carries = call(
        functools.partial(scan_kernel, scale), (), [vmem] * 3, vmem, slabs, limit=SMALL_LIMIT
    )(received, coef_slabs, rate_own)

    returned = exchange(carries)

    gate_in, _ = lax.optimization_barrier((conv, carries))
    gate_block = pl.BlockSpec((tokens, channels // 4), lambda n: (0, n))
    grad_query = call(gate_kernel, (4,), [gate_block] * 2, gate_block, token_half, moved=3 * 2**20)(grad, gate_in)

    coef_part = call(
        total_kernel, (), [vmem], vmem, jax.ShapeDtypeStruct((SUB, LANES), F32), limit=SMALL_LIMIT
    )(returned)
    other = lax.ppermute(coef_part, "dp", [(0, 1), (1, 0)])

    grad_key, grad_value = call(
        output_kernel, steps,
        [token_block, token_block, slab_block, mode_block, mode_block, token_block, token_block],
        [token_block] * 2, [token_half] * 2,
        [table(MODES, WIDTH), table(MODES, WIDTH), table(2, 32, LANES), table(2, TOKENS, LANES)],
        10**9, 9 * 2**20,
    )(near, lead, returned, rates, residue, key, value)

    coef = (coef_part + other)[4:].reshape(MODES, own).T
    return (grad_query[None], grad_key[None], grad_value[None], coef)


def solution(mesh):
    rows = P("dp", "ctx", None)
    return jax.shard_map(
        local,
        mesh=mesh,
        in_specs=(rows, rows, rows, rows, rows, P(), P()),
        out_specs=(rows, rows, rows, P("ctx", None)),
        check_vma=False,
    )
```

```python
import functools
import math

import jax
import jax.numpy as jnp
from jax import lax
from jax.experimental import pallas as pl
from jax.experimental.pallas import tpu as pltpu
from jax.sharding import PartitionSpec as P

F32 = jnp.float32
BF16 = jnp.bfloat16
LANES = 128
SUB = 8
TOKENS = 128
ROWS = TOKENS // SUB
MODES = 16
QUADS = 4
WIDTH = 1024
VMEM_LIMIT = 60 * 1024 * 1024
SMALL_LIMIT = 4 * 1024 * 1024
STREAM_LIMIT = 40 * 1024 * 1024


def lane_slice(tile):
    return pl.ds(pl.multiple_of(tile * LANES, LANES), LANES)


def slab_rows(tile):
    return pl.ds(pl.multiple_of(tile * 32, 32), 32)


def gain_of(rates):
    square = rates * rates
    series = 1.0 + square * (1.0 / 6.0 + square * (1.0 / 120.0 + square * (1.0 / 5040.0)))
    return jnp.sqrt(2.0 * rates * series * jnp.exp(-rates))


def wide(row):
    return jnp.broadcast_to(row, (SUB, LANES))


def halves_sum(terms):
    while len(terms) > 1:
        terms = [x + y for x, y in zip(terms[::2], terms[1::2])]
    return terms[0]


def swap_quarters(tile):
    j = lax.broadcasted_iota(jnp.int32, (SUB, LANES), 0) & 3
    q = lax.broadcasted_iota(jnp.int32, (SUB, LANES), 1) >> 5
    for bit in (1, 2):
        j_set = (j & bit) != 0
        q_set = (q & bit) != 0
        up, down = pltpu.roll(tile, bit, 0), pltpu.roll(tile, SUB - bit, 0)
        if bit == 2:
            moved = pltpu.roll(jnp.where(j_set, up, down), 64, 1)
        else:
            moved = jnp.where(j_set, pltpu.roll(up, LANES - 32, 1), pltpu.roll(down, 32, 1))
        tile = jnp.where(j_set == q_set, tile, moved)
    return tile


def natural(tokens_sub, row):
    return tokens_sub[pl.ds(64 * (row % 2) + row // 2, SUB, stride=SUB), :]


def fold(first, second, bit, place):
    clear = (place & bit) == 0
    left = jnp.where(clear, first, pltpu.roll(second, bit, 0))
    right = jnp.where(clear, pltpu.roll(first, SUB - bit, 0), second)
    return left + right


def sublane_sums(tiles, place):
    for bit in (4, 2, 1):
        tiles = [fold(tiles[i], tiles[i + bit], bit, place) for i in range(bit)]
    return tiles[0]


def each_tile(width, body, slots=2):
    def some(at, _):
        for slot in range(slots):
            body(slots * at + slot, slot)
        return 0

    lax.fori_loop(0, width // (slots * LANES), some, 0)


def weighted_sums(state, entry, rows_of, place):
    for bit, power in ((4, 3), (2, 2), (1, 1)):
        clear = (place & bit) == 0
        weights = [rows_of(power, bit, i) for i in range(bit)]
        for which, tiles in enumerate((state, entry)):
            folded = []
            for i, weight in enumerate(weights):
                first, second = tiles[i], tiles[i + bit]
                left = jnp.where(clear, first, pltpu.roll(second, bit, 0))
                right = jnp.where(clear, pltpu.roll(first, SUB - bit, 0), second)
                folded.append(left + weight * right if which == 0 else right + weight * left)
            if which == 0:
                state = folded
            else:
                entry = folded
    return state[0], entry[0]


def summary_kernel(
    grad_ref, query_ref, key_ref, value_ref, rate_ref,
    mixed_ref, product_ref, state_ref, entry_ref, send_ref,
    powers, full,
):
    rates = rate_ref[...]
    for index, power in enumerate((1.0, 16.0, 32.0, 64.0)):
        powers[index] = jnp.exp(-power * rates)
    place = lax.broadcasted_iota(jnp.int32, (SUB, LANES), 0)

    def body(tile, slot):
        lanes = lane_slice(tile)
        mixed_full, product_full = full.at[slot, 0], full.at[slot, 1]
        mixed = (grad_ref[:, lanes].astype(F32) * query_ref[:, lanes].astype(F32)).astype(BF16)
        product = (key_ref[:, lanes].astype(F32) * value_ref[:, lanes].astype(F32)).astype(BF16)
        mixed_full[...] = mixed.astype(F32)
        product_full[...] = product.astype(F32)
        g = [mixed_full[pl.ds(j, SUB, stride=ROWS), :] for j in range(ROWS)]
        p = [product_full[pl.ds(j, SUB, stride=ROWS), :] for j in range(ROWS)]
        for j in range(0, ROWS, 2):
            rows = slice(SUB * j, SUB * j + 16)
            mixed_ref[rows, lanes] = jnp.concatenate([g[j], g[j + 1]], axis=0).astype(BF16)
            product_ref[rows, lanes] = jnp.concatenate([p[j], p[j + 1]], axis=0).astype(BF16)
        sums = []
        for half in range(2):
            states, entries = [], []
            for base in range(SUB * half, SUB * half + SUB, 4):
                group = range(base, base + 4)
                one = [wide(powers[0, m : m + 1, lanes]) for m in group]
                state = [g[ROWS - 1]] * 4
                entry = [p[0] * a for a in one]
                for i in range(1, ROWS):
                    state = [s * a + g[ROWS - 1 - i] for s, a in zip(state, one)]
                    entry = [(e + p[i]) * a for e, a in zip(entry, one)]
                for s, e, m in zip(state, entry, group):
                    state_ref[SUB * m : SUB * m + SUB, lanes] = s
                    entry_ref[SUB * m : SUB * m + SUB, lanes] = e
                states += state
                entries += entry

            def rows_of(power, bit, i):
                if bit == 1:
                    return powers[power, SUB * half : SUB * half + SUB, lanes]
                modes = [SUB * half + i + bit * at for at in range(SUB // bit)]
                out = wide(powers[power, modes[-1] : modes[-1] + 1, lanes])
                for at in range(len(modes) - 2, -1, -1):
                    out = jnp.where(place < bit * (at + 1), wide(powers[power, modes[at] : modes[at] + 1, lanes]), out)
                return out

            s, e = weighted_sums(states, entries, rows_of, place)
            low = place < 4
            sums += [jnp.where(low, s, pltpu.roll(e, 4, 0)), jnp.where(low, pltpu.roll(s, 4, 0), e)]
        send_ref[slab_rows(tile), :] = jnp.concatenate(sums, axis=0).astype(BF16)

    each_tile(grad_ref.shape[1], body)


def local_kernel(
    scale, mixed_ref, product_ref, state_ref, entry_ref, rate_ref, residue_ref,
    near_ref, lead_ref, send_ref,
    powers, weights, taps, lags, slabs, runs,
):
    rates = rate_ref[...]
    powers[...] = jnp.exp(-rates)
    gains = gain_of(rates)
    term = residue_ref[...] * gains
    for d in range(ROWS):
        taps[d : d + 1, :] = jnp.sum(term, axis=0, keepdims=True)
        term = term * powers[...]
        if d == 0:
            weights[...] = term
    for index, power in enumerate((16.0, 32.0, 64.0)):
        runs[index] = jnp.exp(-power * rates)
    place = lax.broadcasted_iota(jnp.int32, (SUB, LANES), 0)

    def body(tile, slot):
        lanes = lane_slice(tile)
        g, p = [], []
        for j in range(0, ROWS, 2):
            rows = slice(SUB * j, SUB * j + 16)
            pair = mixed_ref[rows, lanes].astype(F32)
            g += [pair[:SUB, :], pair[SUB:, :]]
            pair = product_ref[rows, lanes].astype(F32)
            p += [pair[:SUB, :], pair[SUB:, :]]
        near = [None] * ROWS
        for d in range(ROWS):
            tap = wide(taps[d : d + 1, lanes])
            for j in range(ROWS - d):
                near[j] = tap * g[j + d] if d == 0 else near[j] + tap * g[j + d]
        for j in range(ROWS):
            near_ref[SUB * j : SUB * j + SUB, lanes] = near[j]
        lag = []
        for d in range(ROWS):
            total = g[d] * p[0]
            for j in range(1, ROWS - d):
                total = total + g[j + d] * p[j]
            lag.append(total)
        for half in range(2):
            rows = slice(SUB * half, SUB * half + SUB)
            lags[0, rows, lanes] = sublane_sums(lag[rows], place)
            cross = []
            for m in range(SUB * half, SUB * half + SUB):
                mode_rows = slice(SUB * m, SUB * m + SUB)
                carry = state_ref[mode_rows, lanes]
                for index, step in ((0, 1), (1, 2), (2, 4)):
                    later = jnp.where(place < SUB - step, pltpu.roll(carry, SUB - step, 0), 0.0)
                    carry = carry + wide(runs[index, m : m + 1, lanes]) * later
                carry = jnp.where(place < SUB - 1, pltpu.roll(carry, SUB - 1, 0), 0.0)
                cross.append(carry * entry_ref[mode_rows, lanes])
                lead_ref[mode_rows, lanes] = carry * wide(weights[m : m + 1, lanes])
            lags[1, rows, lanes] = sublane_sums(cross, place)

    each_tile(mixed_ref.shape[1], body)
    coef = jnp.broadcast_to(lags[0, ROWS - 1 : ROWS, :], rates.shape)
    for d in range(ROWS - 2, -1, -1):
        coef = coef * powers[...] + lags[0, d : d + 1, :]
    lags[1] = (coef + lags[1]) * gains * scale
    slabs[...] = jnp.zeros_like(slabs)

    def ship(tile, slot):
        lanes = lane_slice(tile)
        slab = slabs.at[slot]
        for pair in range(2):
            moved = swap_quarters(lags[1, SUB * pair : SUB * pair + SUB, lanes])
            for k in range(2):
                for q in range(4):
                    row = SUB * q + 4 + 2 * pair + k
                    slab[row : row + 1, :] = moved[4 * k + q : 4 * k + q + 1, :]
        send_ref[slab_rows(tile), :] = slab[...].astype(BF16)

    each_tile(mixed_ref.shape[1], ship, 8)


def scan_kernel(scale, received_ref, coef_ref, rate_ref, send_ref):
    blocks = received_ref.shape[0] // SUB
    rates = rate_ref[...]
    decay = jnp.exp(-float(TOKENS) * rates)
    place = lax.broadcasted_iota(jnp.int32, (SUB, LANES), 0)
    low = place < 4

    def step(back, held):
        state, far = held
        start = pl.multiple_of((blocks // 2 - 1 - back) * 16, 16)
        pair = received_ref[pl.ds(start, 16), :].astype(F32)
        coef = coef_ref[pl.ds(start, 16), :].astype(F32)
        out = [None, None]
        for which in (1, 0):
            here = pair[SUB * which : SUB * which + SUB, :]
            out[which] = jnp.where(low, state, coef[SUB * which : SUB * which + SUB, :])
            far = far + here * state
            state = jnp.where(low, here, pltpu.roll(here, 4, 0)) + decay * state
        send_ref[pl.ds(start, 16), :] = jnp.concatenate(out, axis=0).astype(BF16)
        return state, far

    zero = jnp.zeros((SUB, LANES), F32)
    _, far = lax.fori_loop(0, blocks // 2, step, (zero, zero), unroll=4)
    far = swap_quarters(far * gain_of(rates) * scale)
    me = lax.axis_index("ctx")
    mine = slab_rows(me // QUADS)
    extra = [jnp.where(place == 4 + me % QUADS, wide(far[4 + q : 5 + q, :]), 0.0) for q in range(QUADS)]
    send_ref[mine, :] = (send_ref[mine, :].astype(F32) + jnp.concatenate(extra, axis=0)).astype(BF16)


def total_kernel(received_ref, out_ref):
    def step(at, held):
        rows = received_ref[pl.ds(pl.multiple_of(at * 16, 16), 16), :].astype(F32)
        return held[0] + rows[:SUB, :], held[1] + rows[SUB:, :]

    zero = jnp.zeros((SUB, LANES), F32)
    first, second = lax.fori_loop(0, received_ref.shape[0] // 16, step, (zero, zero), unroll=8)
    total = first + second
    width = out_ref.shape[1]
    for k in range(QUADS):
        for j in range(4):
            out_ref[4 * k + j : 4 * k + j + 1, :] = total[4 + k : 5 + k, width * j : width * j + width]


def stage_kernel(
    rate_far, residue_far, near_far, lead_far, key_far, value_far,
    reach_far, power_far, near_head, lead_head, reach_head, power_head, key_head, value_head,
    rate_ref, residue_ref, reach_ref, power_ref, weights, sems,
):
    width = near_head.shape[1]
    pairs = [(rate_far, rate_ref), (residue_far, residue_ref)]
    heads = ((near_far, near_head), (lead_far, lead_head), (key_far, key_head), (value_far, value_head))
    pairs += [(far.at[:, pl.ds(0, width)], head) for far, head in heads]
    coming = [pltpu.make_async_copy(*pair, sems.at[i]) for i, pair in enumerate(pairs)]
    for each in coming:
        each.start()
    for each in coming[:2]:
        each.wait()
    power_ref[...] = jnp.exp(-rate_ref[...])
    weights[...] = residue_ref[...] * gain_of(rate_ref[...]) * power_ref[...]
    back = (16 * (SUB - 1 - lax.broadcasted_iota(jnp.int32, (SUB, LANES), 0))).astype(F32)

    def body(tile, slot):
        lanes = lane_slice(tile)
        for m in range(MODES):
            reach = jnp.exp(-back * wide(rate_ref[m : m + 1, lanes]))
            reach_ref[SUB * m : SUB * m + SUB, lanes] = reach * wide(weights[m : m + 1, lanes])

    each_tile(rate_ref.shape[1], body)
    going = [
        pltpu.make_async_copy(reach_ref, reach_far, sems.at[len(pairs)]),
        pltpu.make_async_copy(power_ref, power_far, sems.at[len(pairs) + 1]),
    ]
    for each in going:
        each.start()
    reach_head[...] = reach_ref[:, :width]
    power_head[...] = power_ref[:, :width]
    for each in coming[2:] + going:
        each.wait()


def output_kernel(
    near_ref, lead_ref, reach_ref, power_ref, key_ref, value_ref, received_ref,
    grad_key_ref, grad_value_ref,
    slabs, mixes,
):
    def body(tile, slot):
        lanes = lane_slice(tile)
        slab, mix_sub = slabs.at[slot], mixes.at[slot]
        slab[...] = received_ref[slab_rows(tile), :].astype(F32)
        one = [wide(power_ref[m : m + 1, lanes]) for m in range(MODES)]
        state = []
        for m in range(MODES):
            row = SUB * (m // 4) + m % 4
            rows = slice(SUB * m, SUB * m + SUB)
            state.append(lead_ref[rows, lanes] + wide(slab[row : row + 1, :]) * reach_ref[rows, lanes])
        for j in range(ROWS - 1, -1, -1):
            rows = slice(SUB * j, SUB * j + SUB)
            mix_sub[rows, :] = near_ref[rows, lanes] + halves_sum(state)
            if j > 0:
                state = [s * a for s, a in zip(state, one)]
        for i in range(0, ROWS, 2):
            rows = slice(SUB * i, SUB * i + 16)
            mix = jnp.concatenate([natural(mix_sub, i), natural(mix_sub, i + 1)], axis=0).astype(BF16).astype(F32)
            grad_key_ref[rows, lanes] = (mix * value_ref[rows, lanes].astype(F32)).astype(BF16)
            grad_value_ref[rows, lanes] = (mix * key_ref[rows, lanes].astype(F32)).astype(BF16)

    each_tile(near_ref.shape[1], body)


def gate_kernel(grad_ref, conv_ref, out_ref):
    def body(tile, slot):
        lanes = lane_slice(tile)
        out_ref[:, lanes] = (grad_ref[:, lanes].astype(F32) * conv_ref[:, lanes].astype(F32)).astype(BF16)

    each_tile(grad_ref.shape[1], body)


def streamed(body, ins, outs, width, scratch, flops, moved, heads=(), ahead=3):
    arrays = [x for x, _ in ins + outs]
    n_in, n_all = len(ins), len(ins) + len(outs)
    stays = [kept for _, kept in ins + outs]
    steps = max(x.shape[1] for x in arrays) // width
    moving = [i for i in range(n_all) if not stays[i]]
    first = 1 if heads else 0

    def block(ref, at):
        if ref.shape[1] == LANES:
            size = width // LANES * 32
            return ref.at[pl.ds(pl.multiple_of(at * size, size), size), :]
        return ref.at[:, pl.ds(pl.multiple_of(at * width, width), width)]

    def kernel(*refs):
        ready = refs[n_in : n_in + len(heads)]
        refs = refs[:n_in] + refs[n_in + len(heads) :]
        places = dict(zip(moving, refs[n_all : n_all + len(moving)]))
        sems, *extra = refs[n_all + len(moving) :]

        def copy(i, at):
            ends = (block(refs[i], at), block(places[i], at))
            return pltpu.make_async_copy(*(ends if i < n_in else ends[::-1]), sems.at[i, at])

        coming = [i for i in moving if i < n_in]
        going = [i for i in moving if i >= n_in]
        for at in range(first, min(first + ahead, steps)):
            for i in coming:
                copy(i, at).start()

        def work(at, held):
            body(*(held.get(i, block(places.get(i, refs[i]), at)) for i in range(n_all)), *extra)
            for i in going:
                copy(i, at).start()

        def step(at, _):
            @pl.when(at + ahead < steps)
            def _():
                for i in coming:
                    copy(i, at + ahead).start()

            for i in coming:
                copy(i, at).wait()
            work(at, {})
            return 0

        if heads:
            work(0, dict(zip(coming, ready)))
        lax.fori_loop(first, steps, step, 0)
        for at in range(steps):
            for i in going:
                copy(i, at).wait()

    space = [pltpu.VMEM if kept else pltpu.HBM for kept in stays]
    specs = [pl.BlockSpec(memory_space=kind) for kind in space]
    held = [pltpu.with_memory_space_constraint(x, kind) for x, kind in zip(arrays[:n_in], space)]
    held += [pltpu.with_memory_space_constraint(x, pltpu.VMEM) for x in heads]
    results = [kind(x.shape, x.dtype) for x, kind in zip(arrays[n_in:], space[n_in:])]
    return call(
        kernel, (), specs[:n_in] + [pl.BlockSpec(memory_space=pltpu.VMEM)] * len(heads), specs[n_in:], results,
        [pltpu.VMEM(arrays[i].shape, arrays[i].dtype) for i in moving]
        + [pltpu.SemaphoreType.DMA((n_all, steps))]
        + scratch,
        flops, moved, STREAM_LIMIT,
    )(*held)


def call(kernel, grid, in_specs, out_specs, out_shape, scratch=(), flops=10**6, moved=2**20, limit=VMEM_LIMIT):
    return pl.pallas_call(
        kernel,
        grid=grid,
        in_specs=in_specs,
        out_specs=out_specs,
        out_shape=out_shape,
        scratch_shapes=scratch,
        compiler_params=pltpu.CompilerParams(vmem_limit_bytes=limit),
        cost_estimate=pl.CostEstimate(flops=flops, bytes_accessed=moved, transcendentals=0),
    )


def local(query_rows, key_rows, value_rows, conv_rows, grad_rows, residues, decay_rates):
    blocks = lax.axis_size("ctx")
    tokens, channels = query_rows.shape[1:]
    own = channels // blocks
    scale = 1.0 / math.sqrt(blocks * tokens)
    query, key, value, conv, grad = (x[0] for x in (query_rows, key_rows, value_rows, conv_rows, grad_rows))
    rates, residue = decay_rates.T, residues.T

    def table(*shape):
        return pltpu.VMEM(shape, F32)

    token_block = pl.BlockSpec((tokens, WIDTH), lambda n: (0, n))
    mode_block = pl.BlockSpec((MODES, WIDTH), lambda n: (0, n))
    slab_block = pl.BlockSpec((WIDTH // LANES * 32, LANES), lambda n: (n, 0))
    token_half = jax.ShapeDtypeStruct((tokens, channels), BF16)
    token_full = jax.ShapeDtypeStruct((tokens, channels), F32)
    slabs = jax.ShapeDtypeStruct((blocks * SUB, LANES), BF16)
    steps = (channels // WIDTH,)

    mixed, product, states, entries, summary = call(
        summary_kernel, steps,
        [token_block] * 4 + [mode_block],
        [token_block] * 4 + [slab_block],
        [token_half, token_half, token_full, token_full, slabs],
        [table(4, MODES, WIDTH), table(2, 2, TOKENS, LANES)],
        10**9, 10 * 2**20,
    )(grad, query, key, value, rates)

    def exchange(rows):
        moved = lax.all_to_all(rows.reshape(blocks, SUB, LANES), "ctx", split_axis=0, concat_axis=0, tiled=True)
        return moved.reshape(blocks * SUB, LANES)

    received = exchange(summary)

    near, lead, coef_slabs = streamed(
        functools.partial(local_kernel, scale),
        [(x, False) for x in (mixed, product, states, entries, rates, residue)],
        [(token_full, False), (token_full, False), (slabs, True)],
        WIDTH,
        [
            table(MODES, WIDTH), table(MODES, WIDTH), table(MODES, WIDTH), table(2, MODES, WIDTH),
            table(8, 32, LANES), table(3, MODES, WIDTH),
        ],
        10**9, 10 * 2**20,
    )

    me = lax.axis_index("ctx")
    rates_late, _ = lax.optimization_barrier((rates, summary))
    rate_own = lax.dynamic_slice(rates_late, (4 * (me % QUADS), LANES * (me // QUADS)), (4, LANES))
    rate_own = jnp.concatenate([rate_own, rate_own], axis=0)

    vmem = pl.BlockSpec(memory_space=pltpu.VMEM)
    carries = call(
        functools.partial(scan_kernel, scale), (), [vmem] * 3, vmem, slabs, limit=SMALL_LIMIT
    )(received, coef_slabs, rate_own)

    returned = exchange(carries)

    gate_in, key_late, value_late, _ = lax.optimization_barrier((conv, key, value, carries))
    far_spec, near_spec = pl.BlockSpec(memory_space=pltpu.HBM), pl.BlockSpec(memory_space=pltpu.VMEM)
    head_types = [pltpu.VMEM((x.shape[0], WIDTH), x.dtype) for x in (near, lead, near, rates, key, value)]
    reach, power, *heads = call(
        stage_kernel, (), [far_spec] * 6, [far_spec] * 2 + [near_spec] * 6,
        [pltpu.HBM(near.shape, F32), pltpu.HBM(rates.shape, F32)] + head_types,
        [pltpu.VMEM(x.shape, F32) for x in (rates, rates, near, rates, rates)] + [pltpu.SemaphoreType.DMA((8,))],
        10**9, 4 * 2**20, STREAM_LIMIT,
    )(*(pltpu.with_memory_space_constraint(x, pltpu.HBM) for x in (rates, residue, near, lead, key_late, value_late)))
    grad_query = streamed(
        gate_kernel, [(grad, False), (gate_in, False)], [(token_half, False)], WIDTH, [], 10**6, 3 * 2**20
    )[0]

    coef_part = call(
        total_kernel, (), [vmem], vmem, jax.ShapeDtypeStruct((MODES, own), F32), limit=SMALL_LIMIT
    )(returned)
    other = lax.ppermute(coef_part, "dp", [(0, 1), (1, 0)])

    grad_key, grad_value = streamed(
        output_kernel,
        [(x, False) for x in (near, lead, reach, power, key, value)] + [(returned, True)],
        [(token_half, False), (token_half, False)],
        WIDTH,
        [table(2, 32, LANES), table(2, TOKENS, LANES)],
        10**9, 9 * 2**20, heads,
    )

    coef = (coef_part + other).T
    return (grad_query[None], grad_key[None], grad_value[None], coef)


def solution(mesh):
    rows = P("dp", "ctx", None)
    return jax.shard_map(
        local,
        mesh=mesh,
        in_specs=(rows, rows, rows, rows, rows, P(), P()),
        out_specs=(rows, rows, rows, P("ctx", None)),
        check_vma=False,
    )
```

```python
import functools
import math

import jax
import jax.numpy as jnp
from jax import lax
from jax.experimental import pallas as pl
from jax.experimental.pallas import tpu as pltpu
from jax.sharding import PartitionSpec as P

F32 = jnp.float32
BF16 = jnp.bfloat16
LANES = 128
SUB = 8
TOKENS = 128
ROWS = TOKENS // SUB
MODES = 16
QUADS = 4
WIDTH = 1024
VMEM_LIMIT = 60 * 1024 * 1024
SMALL_LIMIT = 4 * 1024 * 1024
STREAM_LIMIT = 40 * 1024 * 1024


def lane_slice(tile):
    return pl.ds(pl.multiple_of(tile * LANES, LANES), LANES)


def slab_rows(tile):
    return pl.ds(pl.multiple_of(tile * 32, 32), 32)


def gain_of(rates):
    square = rates * rates
    series = 1.0 + square * (1.0 / 6.0 + square * (1.0 / 120.0 + square * (1.0 / 5040.0)))
    return jnp.sqrt(2.0 * rates * series * jnp.exp(-rates))


def wide(row):
    return jnp.broadcast_to(row, (SUB, LANES))


def halves_sum(terms):
    while len(terms) > 1:
        terms = [x + y for x, y in zip(terms[::2], terms[1::2])]
    return terms[0]


def swap_quarters(tile):
    j = lax.broadcasted_iota(jnp.int32, (SUB, LANES), 0) & 3
    q = lax.broadcasted_iota(jnp.int32, (SUB, LANES), 1) >> 5
    for bit in (1, 2):
        j_set = (j & bit) != 0
        q_set = (q & bit) != 0
        up, down = pltpu.roll(tile, bit, 0), pltpu.roll(tile, SUB - bit, 0)
        if bit == 2:
            moved = pltpu.roll(jnp.where(j_set, up, down), 64, 1)
        else:
            moved = jnp.where(j_set, pltpu.roll(up, LANES - 32, 1), pltpu.roll(down, 32, 1))
        tile = jnp.where(j_set == q_set, tile, moved)
    return tile


def natural(tokens_sub, row):
    return tokens_sub[pl.ds(64 * (row % 2) + row // 2, SUB, stride=SUB), :]


def fold(first, second, bit, place):
    clear = (place & bit) == 0
    left = jnp.where(clear, first, pltpu.roll(second, bit, 0))
    right = jnp.where(clear, pltpu.roll(first, SUB - bit, 0), second)
    return left + right


def sublane_sums(tiles, place):
    for bit in (4, 2, 1):
        tiles = [fold(tiles[i], tiles[i + bit], bit, place) for i in range(bit)]
    return tiles[0]


def each_tile(width, body, slots=2):
    def some(at, _):
        for slot in range(slots):
            body(slots * at + slot, slot)
        return 0

    lax.fori_loop(0, width // (slots * LANES), some, 0)


def weighted_sums(state, entry, rows_of, place):
    for bit, power in ((4, 3), (2, 2), (1, 1)):
        clear = (place & bit) == 0
        weights = [rows_of(power, bit, i) for i in range(bit)]
        for which, tiles in enumerate((state, entry)):
            folded = []
            for i, weight in enumerate(weights):
                first, second = tiles[i], tiles[i + bit]
                left = jnp.where(clear, first, pltpu.roll(second, bit, 0))
                right = jnp.where(clear, pltpu.roll(first, SUB - bit, 0), second)
                folded.append(left + weight * right if which == 0 else right + weight * left)
            if which == 0:
                state = folded
            else:
                entry = folded
    return state[0], entry[0]


def summary_kernel(
    grad_ref, query_ref, key_ref, value_ref, rate_ref,
    mixed_ref, product_ref, state_ref, entry_ref, send_ref,
    powers, full,
):
    rates = rate_ref[...]
    for index, power in enumerate((1.0, 16.0, 32.0, 64.0)):
        powers[index] = jnp.exp(-power * rates)
    place = lax.broadcasted_iota(jnp.int32, (SUB, LANES), 0)

    def body(tile, slot):
        lanes = lane_slice(tile)
        mixed_full, product_full = full.at[slot, 0], full.at[slot, 1]
        mixed = (grad_ref[:, lanes].astype(F32) * query_ref[:, lanes].astype(F32)).astype(BF16)
        product = (key_ref[:, lanes].astype(F32) * value_ref[:, lanes].astype(F32)).astype(BF16)
        mixed_full[...] = mixed.astype(F32)
        product_full[...] = product.astype(F32)
        g = [mixed_full[pl.ds(j, SUB, stride=ROWS), :] for j in range(ROWS)]
        p = [product_full[pl.ds(j, SUB, stride=ROWS), :] for j in range(ROWS)]
        for j in range(0, ROWS, 2):
            rows = slice(SUB * j, SUB * j + 16)
            mixed_ref[rows, lanes] = jnp.concatenate([g[j], g[j + 1]], axis=0).astype(BF16)
            product_ref[rows, lanes] = jnp.concatenate([p[j], p[j + 1]], axis=0).astype(BF16)
        sums = []
        for half in range(2):
            states, entries = [], []
            for base in range(SUB * half, SUB * half + SUB, 4):
                group = range(base, base + 4)
                one = [wide(powers[0, m : m + 1, lanes]) for m in group]
                state = [g[ROWS - 1]] * 4
                entry = [p[0] * a for a in one]
                for i in range(1, ROWS):
                    state = [s * a + g[ROWS - 1 - i] for s, a in zip(state, one)]
                    entry = [(e + p[i]) * a for e, a in zip(entry, one)]
                for s, e, m in zip(state, entry, group):
                    state_ref[SUB * m : SUB * m + SUB, lanes] = s
                    entry_ref[SUB * m : SUB * m + SUB, lanes] = e
                states += state
                entries += entry

            def rows_of(power, bit, i):
                if bit == 1:
                    return powers[power, SUB * half : SUB * half + SUB, lanes]
                modes = [SUB * half + i + bit * at for at in range(SUB // bit)]
                out = wide(powers[power, modes[-1] : modes[-1] + 1, lanes])
                for at in range(len(modes) - 2, -1, -1):
                    out = jnp.where(place < bit * (at + 1), wide(powers[power, modes[at] : modes[at] + 1, lanes]), out)
                return out

            s, e = weighted_sums(states, entries, rows_of, place)
            low = place < 4
            sums += [jnp.where(low, s, pltpu.roll(e, 4, 0)), jnp.where(low, pltpu.roll(s, 4, 0), e)]
        send_ref[slab_rows(tile), :] = jnp.concatenate(sums, axis=0).astype(BF16)

    each_tile(grad_ref.shape[1], body)


def local_kernel(
    scale, mixed_ref, product_ref, state_ref, entry_ref, rate_ref, residue_ref,
    lead_ref, send_ref,
    powers, weights, lags, slabs, runs,
):
    rates = rate_ref[...]
    powers[...] = jnp.exp(-rates)
    gains = gain_of(rates)
    weights[...] = residue_ref[...] * gains * powers[...]
    for index, power in enumerate((16.0, 32.0, 64.0)):
        runs[index] = jnp.exp(-power * rates)
    place = lax.broadcasted_iota(jnp.int32, (SUB, LANES), 0)

    def body(tile, slot):
        lanes = lane_slice(tile)
        g, p = [], []
        for j in range(0, ROWS, 2):
            rows = slice(SUB * j, SUB * j + 16)
            pair = mixed_ref[rows, lanes].astype(F32)
            g += [pair[:SUB, :], pair[SUB:, :]]
            pair = product_ref[rows, lanes].astype(F32)
            p += [pair[:SUB, :], pair[SUB:, :]]
        lag = []
        for d in range(ROWS):
            total = g[d] * p[0]
            for j in range(1, ROWS - d):
                total = total + g[j + d] * p[j]
            lag.append(total)
        for half in range(2):
            rows = slice(SUB * half, SUB * half + SUB)
            lags[0, rows, lanes] = sublane_sums(lag[rows], place)
            cross = []
            for m in range(SUB * half, SUB * half + SUB):
                mode_rows = slice(SUB * m, SUB * m + SUB)
                carry = state_ref[mode_rows, lanes]
                for index, step in ((0, 1), (1, 2), (2, 4)):
                    later = jnp.where(place < SUB - step, pltpu.roll(carry, SUB - step, 0), 0.0)
                    carry = carry + wide(runs[index, m : m + 1, lanes]) * later
                carry = jnp.where(place < SUB - 1, pltpu.roll(carry, SUB - 1, 0), 0.0)
                cross.append(carry * entry_ref[mode_rows, lanes])
                lead_ref[mode_rows, lanes] = carry * wide(weights[m : m + 1, lanes])
            lags[1, rows, lanes] = sublane_sums(cross, place)

    each_tile(mixed_ref.shape[1], body)
    coef = jnp.broadcast_to(lags[0, ROWS - 1 : ROWS, :], rates.shape)
    for d in range(ROWS - 2, -1, -1):
        coef = coef * powers[...] + lags[0, d : d + 1, :]
    lags[1] = (coef + lags[1]) * gains * scale
    slabs[...] = jnp.zeros_like(slabs)

    def ship(tile, slot):
        lanes = lane_slice(tile)
        slab = slabs.at[slot]
        for pair in range(2):
            moved = swap_quarters(lags[1, SUB * pair : SUB * pair + SUB, lanes])
            for k in range(2):
                for q in range(4):
                    row = SUB * q + 4 + 2 * pair + k
                    slab[row : row + 1, :] = moved[4 * k + q : 4 * k + q + 1, :]
        send_ref[slab_rows(tile), :] = slab[...].astype(BF16)

    each_tile(mixed_ref.shape[1], ship, 8)


def scan_kernel(scale, received_ref, coef_ref, rate_ref, send_ref):
    blocks = received_ref.shape[0] // SUB
    rates = rate_ref[...]
    decay = jnp.exp(-float(TOKENS) * rates)
    place = lax.broadcasted_iota(jnp.int32, (SUB, LANES), 0)
    low = place < 4

    squared = decay * decay
    gains = gain_of(rates) * scale

    def step(back, held):
        state, far, far_even = held
        start = pl.multiple_of((blocks // 2 - 1 - back) * 16, 16)
        pair = received_ref[pl.ds(start, 16), :].astype(F32)
        coef = coef_ref[pl.ds(start, 16), :].astype(F32)
        even, odd = pair[:SUB, :], pair[SUB:, :]
        odd_own = jnp.where(low, odd, pltpu.roll(odd, 4, 0))
        even_own = jnp.where(low, even, pltpu.roll(even, 4, 0))
        before = odd_own + decay * state
        out = [jnp.where(low, before, coef[:SUB, :]), jnp.where(low, state, coef[SUB:, :])]
        send_ref[pl.ds(start, 16), :] = jnp.concatenate(out, axis=0).astype(BF16)
        return (even_own + decay * odd_own) + squared * state, far + odd * state, far_even + even * before

    zero = jnp.zeros((SUB, LANES), F32)
    _, far, far_even = lax.fori_loop(0, blocks // 2, step, (zero, zero, zero), unroll=8)
    far = swap_quarters((far + far_even) * gains)
    me = lax.axis_index("ctx")
    mine = slab_rows(me // QUADS)
    extra = [jnp.where(place == 4 + me % QUADS, wide(far[4 + q : 5 + q, :]), 0.0) for q in range(QUADS)]
    send_ref[mine, :] = (send_ref[mine, :].astype(F32) + jnp.concatenate(extra, axis=0)).astype(BF16)


def total_kernel(received_ref, out_ref):
    def step(at, held):
        rows = received_ref[pl.ds(pl.multiple_of(at * 16, 16), 16), :].astype(F32)
        return held[0] + rows[:SUB, :], held[1] + rows[SUB:, :]

    zero = jnp.zeros((SUB, LANES), F32)
    first, second = lax.fori_loop(0, received_ref.shape[0] // 16, step, (zero, zero), unroll=8)
    total = first + second
    width = out_ref.shape[1]
    for k in range(QUADS):
        for j in range(4):
            out_ref[4 * k + j : 4 * k + j + 1, :] = total[4 + k : 5 + k, width * j : width * j + width]


def stage_kernel(
    mixed_far, rate_far, residue_far, lead_far, key_far, value_far,
    near_far, reach_far, power_far, near_head, lead_head, reach_head, power_head, key_head, value_head,
    mixed_ref, rate_ref, residue_ref, near_ref, reach_ref, power_ref, weights, taps, sems,
):
    width = near_head.shape[1]
    heads = ((lead_far, lead_head), (key_far, key_head), (value_far, value_head))
    pairs = [(rate_far, rate_ref), (residue_far, residue_ref), (mixed_far, mixed_ref)]
    pairs += [(far.at[:, pl.ds(0, width)], head) for far, head in heads]
    coming = [pltpu.make_async_copy(*pair, sems.at[i]) for i, pair in enumerate(pairs)]
    for each in coming:
        each.start()
    for each in coming[:2]:
        each.wait()
    power_ref[...] = jnp.exp(-rate_ref[...])
    term = residue_ref[...] * gain_of(rate_ref[...])
    for d in range(ROWS):
        taps[d : d + 1, :] = jnp.sum(term, axis=0, keepdims=True)
        term = term * power_ref[...]
        if d == 0:
            weights[...] = term
    back = (16 * (SUB - 1 - lax.broadcasted_iota(jnp.int32, (SUB, LANES), 0))).astype(F32)
    coming[2].wait()

    def body(tile, slot):
        lanes = lane_slice(tile)
        g = []
        for j in range(0, ROWS, 2):
            pair = mixed_ref[SUB * j : SUB * j + 16, lanes].astype(F32)
            g += [pair[:SUB, :], pair[SUB:, :]]
        near = [None] * ROWS
        for d in range(ROWS):
            tap = wide(taps[d : d + 1, lanes])
            for j in range(ROWS - d):
                near[j] = tap * g[j + d] if d == 0 else near[j] + tap * g[j + d]
        for j in range(ROWS):
            near_ref[SUB * j : SUB * j + SUB, lanes] = near[j]
        for m in range(MODES):
            reach = jnp.exp(-back * wide(rate_ref[m : m + 1, lanes]))
            reach_ref[SUB * m : SUB * m + SUB, lanes] = reach * wide(weights[m : m + 1, lanes])

    each_tile(rate_ref.shape[1], body)
    tables = ((near_ref, near_far), (reach_ref, reach_far), (power_ref, power_far))
    going = [pltpu.make_async_copy(*pair, sems.at[len(pairs) + i]) for i, pair in enumerate(tables)]
    for each in going:
        each.start()
    near_head[...] = near_ref[:, :width]
    reach_head[...] = reach_ref[:, :width]
    power_head[...] = power_ref[:, :width]
    for each in coming[3:] + going:
        each.wait()


def output_kernel(
    near_ref, lead_ref, reach_ref, power_ref, key_ref, value_ref, received_ref,
    grad_key_ref, grad_value_ref,
    slabs, mixes,
):
    def body(tile, slot):
        lanes = lane_slice(tile)
        slab, mix_sub = slabs.at[slot], mixes.at[slot]
        slab[...] = received_ref[slab_rows(tile), :].astype(F32)
        one = [wide(power_ref[m : m + 1, lanes]) for m in range(MODES)]
        state = []
        for m in range(MODES):
            row = SUB * (m // 4) + m % 4
            rows = slice(SUB * m, SUB * m + SUB)
            state.append(lead_ref[rows, lanes] + wide(slab[row : row + 1, :]) * reach_ref[rows, lanes])
        for j in range(ROWS - 1, -1, -1):
            rows = slice(SUB * j, SUB * j + SUB)
            mix_sub[rows, :] = near_ref[rows, lanes] + halves_sum(state)
            if j > 0:
                state = [s * a for s, a in zip(state, one)]
        for i in range(0, ROWS, 2):
            rows = slice(SUB * i, SUB * i + 16)
            mix = jnp.concatenate([natural(mix_sub, i), natural(mix_sub, i + 1)], axis=0).astype(BF16).astype(F32)
            grad_key_ref[rows, lanes] = (mix * value_ref[rows, lanes].astype(F32)).astype(BF16)
            grad_value_ref[rows, lanes] = (mix * key_ref[rows, lanes].astype(F32)).astype(BF16)

    each_tile(near_ref.shape[1], body)


def gate_kernel(grad_ref, conv_ref, out_ref):
    def body(tile, slot):
        lanes = lane_slice(tile)
        out_ref[:, lanes] = (grad_ref[:, lanes].astype(F32) * conv_ref[:, lanes].astype(F32)).astype(BF16)

    each_tile(grad_ref.shape[1], body)


def streamed(body, ins, outs, width, scratch, flops, moved, heads=(), ahead=3):
    arrays = [x for x, _ in ins + outs]
    n_in, n_all = len(ins), len(ins) + len(outs)
    stays = [kept for _, kept in ins + outs]
    steps = max(x.shape[1] for x in arrays) // width
    moving = [i for i in range(n_all) if not stays[i]]
    first = 1 if heads else 0

    def block(ref, at):
        if ref.shape[1] == LANES:
            size = width // LANES * 32
            return ref.at[pl.ds(pl.multiple_of(at * size, size), size), :]
        return ref.at[:, pl.ds(pl.multiple_of(at * width, width), width)]

    def kernel(*refs):
        ready = refs[n_in : n_in + len(heads)]
        refs = refs[:n_in] + refs[n_in + len(heads) :]
        places = dict(zip(moving, refs[n_all : n_all + len(moving)]))
        sems, *extra = refs[n_all + len(moving) :]

        def copy(i, at):
            ends = (block(refs[i], at), block(places[i], at))
            return pltpu.make_async_copy(*(ends if i < n_in else ends[::-1]), sems.at[i, at])

        coming = [i for i in moving if i < n_in]
        going = [i for i in moving if i >= n_in]
        for at in range(first, min(first + ahead, steps)):
            for i in coming:
                copy(i, at).start()

        def work(at, held):
            body(*(held.get(i, block(places.get(i, refs[i]), at)) for i in range(n_all)), *extra)
            for i in going:
                copy(i, at).start()

        def step(at, _):
            @pl.when(at + ahead < steps)
            def _():
                for i in coming:
                    copy(i, at + ahead).start()

            for i in coming:
                copy(i, at).wait()
            work(at, {})
            return 0

        if heads:
            work(0, dict(zip(coming, ready)))
        lax.fori_loop(first, steps, step, 0)
        for at in range(steps):
            for i in going:
                copy(i, at).wait()

    space = [pltpu.VMEM if kept else pltpu.HBM for kept in stays]
    specs = [pl.BlockSpec(memory_space=kind) for kind in space]
    held = [pltpu.with_memory_space_constraint(x, kind) for x, kind in zip(arrays[:n_in], space)]
    held += [pltpu.with_memory_space_constraint(x, pltpu.VMEM) for x in heads]
    results = [kind(x.shape, x.dtype) for x, kind in zip(arrays[n_in:], space[n_in:])]
    return call(
        kernel, (), specs[:n_in] + [pl.BlockSpec(memory_space=pltpu.VMEM)] * len(heads), specs[n_in:], results,
        [pltpu.VMEM(arrays[i].shape, arrays[i].dtype) for i in moving]
        + [pltpu.SemaphoreType.DMA((n_all, steps))]
        + scratch,
        flops, moved, STREAM_LIMIT,
    )(*held)


def call(kernel, grid, in_specs, out_specs, out_shape, scratch=(), flops=10**6, moved=2**20, limit=VMEM_LIMIT):
    return pl.pallas_call(
        kernel,
        grid=grid,
        in_specs=in_specs,
        out_specs=out_specs,
        out_shape=out_shape,
        scratch_shapes=scratch,
        compiler_params=pltpu.CompilerParams(vmem_limit_bytes=limit),
        cost_estimate=pl.CostEstimate(flops=flops, bytes_accessed=moved, transcendentals=0),
    )


def local(query_rows, key_rows, value_rows, conv_rows, grad_rows, residues, decay_rates):
    blocks = lax.axis_size("ctx")
    tokens, channels = query_rows.shape[1:]
    own = channels // blocks
    scale = 1.0 / math.sqrt(blocks * tokens)
    query, key, value, conv, grad = (x[0] for x in (query_rows, key_rows, value_rows, conv_rows, grad_rows))
    rates, residue = decay_rates.T, residues.T

    def table(*shape):
        return pltpu.VMEM(shape, F32)

    token_block = pl.BlockSpec((tokens, WIDTH), lambda n: (0, n))
    mode_block = pl.BlockSpec((MODES, WIDTH), lambda n: (0, n))
    slab_block = pl.BlockSpec((WIDTH // LANES * 32, LANES), lambda n: (n, 0))
    token_half = jax.ShapeDtypeStruct((tokens, channels), BF16)
    token_full = jax.ShapeDtypeStruct((tokens, channels), F32)
    slabs = jax.ShapeDtypeStruct((blocks * SUB, LANES), BF16)
    steps = (channels // WIDTH,)

    mixed, product, states, entries, summary = call(
        summary_kernel, steps,
        [token_block] * 4 + [mode_block],
        [token_block] * 4 + [slab_block],
        [token_half, token_half, token_full, token_full, slabs],
        [table(4, MODES, WIDTH), table(2, 2, TOKENS, LANES)],
        10**9, 10 * 2**20,
    )(grad, query, key, value, rates)

    def exchange(rows):
        moved = lax.all_to_all(rows.reshape(blocks, SUB, LANES), "ctx", split_axis=0, concat_axis=0, tiled=True)
        return moved.reshape(blocks * SUB, LANES)

    received = exchange(summary)

    lead, coef_slabs = streamed(
        functools.partial(local_kernel, scale),
        [(x, False) for x in (mixed, product, states, entries, rates, residue)],
        [(token_full, False), (slabs, True)],
        WIDTH,
        [
            table(MODES, WIDTH), table(MODES, WIDTH), table(2, MODES, WIDTH),
            table(8, 32, LANES), table(3, MODES, WIDTH),
        ],
        10**9, 10 * 2**20,
    )

    me = lax.axis_index("ctx")
    rates_late, _ = lax.optimization_barrier((rates, summary))
    rate_own = lax.dynamic_slice(rates_late, (4 * (me % QUADS), LANES * (me // QUADS)), (4, LANES))
    rate_own = jnp.concatenate([rate_own, rate_own], axis=0)

    vmem = pl.BlockSpec(memory_space=pltpu.VMEM)
    carries = call(
        functools.partial(scan_kernel, scale), (), [vmem] * 3, vmem, slabs, limit=SMALL_LIMIT
    )(received, coef_slabs, rate_own)

    returned = exchange(carries)

    gate_in, key_late, value_late, mixed_late, _ = lax.optimization_barrier((conv, key, value, mixed, carries))
    far_spec, near_spec = pl.BlockSpec(memory_space=pltpu.HBM), pl.BlockSpec(memory_space=pltpu.VMEM)
    head_types = [pltpu.VMEM((x.shape[0], WIDTH), x.dtype) for x in (lead, lead, lead, rates, key, value)]
    near, reach, power, *heads = call(
        stage_kernel, (), [far_spec] * 6, [far_spec] * 3 + [near_spec] * 6,
        [pltpu.HBM(x.shape, F32) for x in (lead, lead, rates)] + head_types,
        [pltpu.VMEM(mixed.shape, BF16)]
        + [pltpu.VMEM(x.shape, F32) for x in (rates, rates, lead, lead, rates, rates, rates)]
        + [pltpu.SemaphoreType.DMA((9,))],
        10**9, 4 * 2**20, STREAM_LIMIT,
    )(*(
        pltpu.with_memory_space_constraint(x, pltpu.HBM)
        for x in (mixed_late, rates, residue, lead, key_late, value_late)
    ))
    grad_query = streamed(
        gate_kernel, [(grad, False), (gate_in, False)], [(token_half, False)], WIDTH, [], 10**6, 3 * 2**20
    )[0]

    coef_part = call(
        total_kernel, (), [vmem], vmem, jax.ShapeDtypeStruct((MODES, own), F32), limit=SMALL_LIMIT
    )(returned)
    other = lax.ppermute(coef_part, "dp", [(0, 1), (1, 0)])

    grad_key, grad_value = streamed(
        output_kernel,
        [(x, False) for x in (near, lead, reach, power, key, value)] + [(returned, True)],
        [(token_half, False), (token_half, False)],
        WIDTH,
        [table(2, 32, LANES), table(2, TOKENS, LANES)],
        10**9, 9 * 2**20, heads,
    )

    coef = (coef_part + other).T
    return (grad_query[None], grad_key[None], grad_value[None], coef)


def solution(mesh):
    rows = P("dp", "ctx", None)
    return jax.shard_map(
        local,
        mesh=mesh,
        in_specs=(rows, rows, rows, rows, rows, P(), P()),
        out_specs=(rows, rows, rows, P("ctx", None)),
        check_vma=False,
    )
```

```python
import functools
import math

import jax
import jax.numpy as jnp
from jax import lax
from jax.experimental import pallas as pl
from jax.experimental.pallas import tpu as pltpu
from jax.sharding import PartitionSpec as P

F32 = jnp.float32
BF16 = jnp.bfloat16
LANES = 128
SUB = 8
TOKENS = 128
ROWS = TOKENS // SUB
MODES = 16
QUADS = 4
PITCH = 24
WIDTH = 1024
VMEM_LIMIT = 60 * 1024 * 1024
SMALL_LIMIT = 4 * 1024 * 1024
STREAM_LIMIT = 40 * 1024 * 1024


def lane_slice(tile):
    return pl.ds(pl.multiple_of(tile * LANES, LANES), LANES)


def slab_rows(tile, tiles):
    return pl.ds(pl.multiple_of((tiles - 1 - tile) * 32, 32), 32)


def gain_of(rates):
    square = rates * rates
    series = 1.0 + square * (1.0 / 6.0 + square * (1.0 / 120.0 + square * (1.0 / 5040.0)))
    return jnp.sqrt(2.0 * rates * series * jnp.exp(-rates))


def wide(row):
    return jnp.broadcast_to(row, (SUB, LANES))


def halves_sum(terms):
    while len(terms) > 1:
        terms = [x + y for x, y in zip(terms[::2], terms[1::2])]
    return terms[0]


def swap_quarters(tile):
    j = lax.broadcasted_iota(jnp.int32, (SUB, LANES), 0) & 3
    q = lax.broadcasted_iota(jnp.int32, (SUB, LANES), 1) >> 5
    for bit in (1, 2):
        j_set = (j & bit) != 0
        q_set = (q & bit) != 0
        up, down = pltpu.roll(tile, bit, 0), pltpu.roll(tile, SUB - bit, 0)
        if bit == 2:
            moved = pltpu.roll(jnp.where(j_set, up, down), 64, 1)
        else:
            moved = jnp.where(j_set, pltpu.roll(up, LANES - 32, 1), pltpu.roll(down, 32, 1))
        tile = jnp.where(j_set == q_set, tile, moved)
    return tile


def natural(tokens_sub, row):
    return tokens_sub[pl.ds(64 * (row % 2) + row // 2, SUB, stride=SUB), :]


def fold(first, second, bit, place):
    clear = (place & bit) == 0
    left = jnp.where(clear, first, pltpu.roll(second, bit, 0))
    right = jnp.where(clear, pltpu.roll(first, SUB - bit, 0), second)
    return left + right


def sublane_sums(tiles, place):
    for bit in (4, 2, 1):
        tiles = [fold(tiles[i], tiles[i + bit], bit, place) for i in range(bit)]
    return tiles[0]


def each_tile(width, body, slots=2):
    def some(at, _):
        for slot in range(slots):
            body(slots * at + slot, slot)
        return 0

    lax.fori_loop(0, width // (slots * LANES), some, 0)


def weighted_sums(state, entry, rows_of, place):
    for bit, power in ((4, 3), (2, 2), (1, 1)):
        clear = (place & bit) == 0
        weights = [rows_of(power, bit, i) for i in range(bit)]
        for which, tiles in enumerate((state, entry)):
            folded = []
            for i, weight in enumerate(weights):
                first, second = tiles[i], tiles[i + bit]
                left = jnp.where(clear, first, pltpu.roll(second, bit, 0))
                right = jnp.where(clear, pltpu.roll(first, SUB - bit, 0), second)
                folded.append(left + weight * right if which == 0 else right + weight * left)
            if which == 0:
                state = folded
            else:
                entry = folded
    return state[0], entry[0]


def summary_kernel(
    grad_ref, query_ref, key_ref, value_ref, rate_ref,
    mixed_ref, product_ref, state_ref, entry_ref, send_ref,
    powers, full,
):
    rates = rate_ref[...]
    for index, power in enumerate((1.0, 16.0, 32.0, 64.0)):
        powers[index] = jnp.exp(-power * rates)
    place = lax.broadcasted_iota(jnp.int32, (SUB, LANES), 0)

    def body(tile, slot):
        lanes = lane_slice(tile)
        mixed_full, product_full = full.at[slot, 0], full.at[slot, 1]
        mixed = (grad_ref[:, lanes].astype(F32) * query_ref[:, lanes].astype(F32)).astype(BF16)
        product = (key_ref[:, lanes].astype(F32) * value_ref[:, lanes].astype(F32)).astype(BF16)
        mixed, product = mixed.astype(F32), product.astype(F32)
        for i in range(ROWS):
            at, rows = PITCH * (i // 2) + SUB * (i % 2), slice(SUB * i, SUB * i + SUB)
            mixed_full[at : at + SUB, :] = mixed[rows, :]
            product_full[at : at + SUB, :] = product[rows, :]
        g = [mixed_full[pl.ds(j, SUB, stride=PITCH), :] for j in range(ROWS)]
        p = [product_full[pl.ds(j, SUB, stride=PITCH), :] for j in range(ROWS)]
        for j in range(0, ROWS, 2):
            rows = slice(SUB * j, SUB * j + 16)
            mixed_ref[rows, lanes] = jnp.concatenate([g[j], g[j + 1]], axis=0).astype(BF16)
            product_ref[rows, lanes] = jnp.concatenate([p[j], p[j + 1]], axis=0).astype(BF16)
        sums = []
        for half in range(2):
            states, entries = [], []
            for base in range(SUB * half, SUB * half + SUB, 4):
                group = range(base, base + 4)
                one = [wide(powers[0, m : m + 1, lanes]) for m in group]
                state = [g[ROWS - 1]] * 4
                entry = [p[0] * a for a in one]
                for i in range(1, ROWS):
                    state = [s * a + g[ROWS - 1 - i] for s, a in zip(state, one)]
                    entry = [(e + p[i]) * a for e, a in zip(entry, one)]
                for s, e, m in zip(state, entry, group):
                    state_ref[SUB * m : SUB * m + SUB, lanes] = s
                    entry_ref[SUB * m : SUB * m + SUB, lanes] = e
                states += state
                entries += entry

            def rows_of(power, bit, i):
                if bit == 1:
                    return powers[power, SUB * half : SUB * half + SUB, lanes]
                modes = [SUB * half + i + bit * at for at in range(SUB // bit)]
                out = wide(powers[power, modes[-1] : modes[-1] + 1, lanes])
                for at in range(len(modes) - 2, -1, -1):
                    out = jnp.where(place < bit * (at + 1), wide(powers[power, modes[at] : modes[at] + 1, lanes]), out)
                return out

            s, e = weighted_sums(states, entries, rows_of, place)
            low = place < 4
            sums += [jnp.where(low, s, pltpu.roll(e, 4, 0)), jnp.where(low, pltpu.roll(s, 4, 0), e)]
        rows = slab_rows(tile, grad_ref.shape[1] // LANES)
        send_ref[rows, :] = jnp.concatenate(sums[::-1], axis=0).astype(BF16)

    each_tile(grad_ref.shape[1], body)


def local_kernel(
    scale, mixed_ref, product_ref, state_ref, entry_ref, rate_ref, residue_ref,
    lead_ref, send_ref,
    powers, weights, lags, slabs, runs,
):
    rates = rate_ref[...]
    powers[...] = jnp.exp(-rates)
    gains = gain_of(rates)
    weights[...] = residue_ref[...] * gains * powers[...]
    for index, power in enumerate((16.0, 32.0, 64.0)):
        runs[index] = jnp.exp(-power * rates)
    place = lax.broadcasted_iota(jnp.int32, (SUB, LANES), 0)

    def body(tile, slot):
        lanes = lane_slice(tile)
        g, p = [], []
        for j in range(0, ROWS, 2):
            rows = slice(SUB * j, SUB * j + 16)
            pair = mixed_ref[rows, lanes].astype(F32)
            g += [pair[:SUB, :], pair[SUB:, :]]
            pair = product_ref[rows, lanes].astype(F32)
            p += [pair[:SUB, :], pair[SUB:, :]]
        lag = []
        for d in range(ROWS):
            total = g[d] * p[0]
            for j in range(1, ROWS - d):
                total = total + g[j + d] * p[j]
            lag.append(total)
        for half in range(2):
            rows = slice(SUB * half, SUB * half + SUB)
            lags[0, rows, lanes] = sublane_sums(lag[rows], place)
            cross = []
            for m in range(SUB * half, SUB * half + SUB):
                mode_rows = slice(SUB * m, SUB * m + SUB)
                carry = state_ref[mode_rows, lanes]
                for index, step in ((0, 1), (1, 2), (2, 4)):
                    later = jnp.where(place < SUB - step, pltpu.roll(carry, SUB - step, 0), 0.0)
                    carry = carry + wide(runs[index, m : m + 1, lanes]) * later
                carry = jnp.where(place < SUB - 1, pltpu.roll(carry, SUB - 1, 0), 0.0)
                cross.append(carry * entry_ref[mode_rows, lanes])
                lead_ref[mode_rows, lanes] = carry * wide(weights[m : m + 1, lanes])
            lags[1, rows, lanes] = sublane_sums(cross, place)

    each_tile(mixed_ref.shape[1], body)
    coef = jnp.broadcast_to(lags[0, ROWS - 1 : ROWS, :], rates.shape)
    for d in range(ROWS - 2, -1, -1):
        coef = coef * powers[...] + lags[0, d : d + 1, :]
    lags[1] = (coef + lags[1]) * gains * scale
    slabs[...] = jnp.zeros_like(slabs)

    def ship(tile, slot):
        lanes = lane_slice(tile)
        slab = slabs.at[slot]
        for pair in range(2):
            moved = swap_quarters(lags[1, SUB * pair : SUB * pair + SUB, lanes])
            for k in range(2):
                for q in range(4):
                    row = SUB * (QUADS - 1 - q) + 4 + 2 * pair + k
                    slab[row : row + 1, :] = moved[4 * k + q : 4 * k + q + 1, :]
        send_ref[slab_rows(tile, mixed_ref.shape[1] // LANES), :] = slab[...].astype(BF16)

    each_tile(mixed_ref.shape[1], ship, 8)


def scan_kernel(scale, received_ref, coef_ref, rate_ref, send_ref):
    blocks = received_ref.shape[0] // SUB
    rates = rate_ref[...]
    decay = jnp.exp(-float(TOKENS) * rates)
    place = lax.broadcasted_iota(jnp.int32, (SUB, LANES), 0)
    low = place < 4

    squared = decay * decay
    gains = gain_of(rates) * scale

    def step(back, held):
        state, far, far_even = held
        start = pl.multiple_of(back * 16, 16)
        pair = received_ref[pl.ds(start, 16), :].astype(F32)
        coef = coef_ref[pl.ds(start, 16), :].astype(F32)
        odd, even = pair[:SUB, :], pair[SUB:, :]
        odd_own = jnp.where(low, odd, pltpu.roll(odd, 4, 0))
        even_own = jnp.where(low, even, pltpu.roll(even, 4, 0))
        before = odd_own + decay * state
        out = [jnp.where(low, state, coef[:SUB, :]), jnp.where(low, before, coef[SUB:, :])]
        send_ref[pl.ds(start, 16), :] = jnp.concatenate(out, axis=0).astype(BF16)
        return (even_own + decay * odd_own) + squared * state, far + odd * state, far_even + even * before

    zero = jnp.zeros((SUB, LANES), F32)
    _, far, far_even = lax.fori_loop(0, blocks // 2, step, (zero, zero, zero), unroll=8)
    far = swap_quarters((far + far_even) * gains)
    me = lax.axis_index("ctx")
    mine = slab_rows(me // QUADS, blocks // QUADS)
    extra = [jnp.where(place == 4 + me % QUADS, wide(far[4 + q : 5 + q, :]), 0.0) for q in range(QUADS - 1, -1, -1)]
    send_ref[mine, :] = (send_ref[mine, :].astype(F32) + jnp.concatenate(extra, axis=0)).astype(BF16)


def total_kernel(received_ref, out_ref):
    def step(at, held):
        rows = received_ref[pl.ds(pl.multiple_of(at * 16, 16), 16), :].astype(F32)
        return held[0] + rows[:SUB, :], held[1] + rows[SUB:, :]

    zero = jnp.zeros((SUB, LANES), F32)
    first, second = lax.fori_loop(0, received_ref.shape[0] // 16, step, (zero, zero), unroll=8)
    total = first + second
    width = out_ref.shape[1]
    for k in range(QUADS):
        for j in range(4):
            out_ref[4 * k + j : 4 * k + j + 1, :] = total[4 + k : 5 + k, width * j : width * j + width]


def stage_kernel(
    mixed_far, rate_far, residue_far, lead_far, key_far, value_far,
    near_far, reach_far, power_far, near_head, lead_head, reach_head, power_head, key_head, value_head,
    mixed_ref, rate_ref, residue_ref, near_ref, reach_ref, power_ref, weights, taps, sems,
):
    width = near_head.shape[1]
    heads = ((lead_far, lead_head), (key_far, key_head), (value_far, value_head))
    pairs = [(rate_far, rate_ref), (residue_far, residue_ref), (mixed_far, mixed_ref)]
    pairs += [(far.at[:, pl.ds(0, width)], head) for far, head in heads]
    coming = [pltpu.make_async_copy(*pair, sems.at[i]) for i, pair in enumerate(pairs)]
    for each in coming:
        each.start()
    for each in coming[:2]:
        each.wait()
    power_ref[...] = jnp.exp(-rate_ref[...])
    term = residue_ref[...] * gain_of(rate_ref[...])
    for d in range(ROWS):
        taps[d : d + 1, :] = jnp.sum(term, axis=0, keepdims=True)
        term = term * power_ref[...]
        if d == 0:
            weights[...] = term
    back = (16 * (SUB - 1 - lax.broadcasted_iota(jnp.int32, (SUB, LANES), 0))).astype(F32)
    coming[2].wait()

    def body(tile, slot):
        lanes = lane_slice(tile)
        g = []
        for j in range(0, ROWS, 2):
            pair = mixed_ref[SUB * j : SUB * j + 16, lanes].astype(F32)
            g += [pair[:SUB, :], pair[SUB:, :]]
        near = [None] * ROWS
        for d in range(ROWS):
            tap = wide(taps[d : d + 1, lanes])
            for j in range(ROWS - d):
                near[j] = tap * g[j + d] if d == 0 else near[j] + tap * g[j + d]
        for j in range(ROWS):
            near_ref[SUB * j : SUB * j + SUB, lanes] = near[j]
        for m in range(MODES):
            reach = jnp.exp(-back * wide(rate_ref[m : m + 1, lanes]))
            reach_ref[SUB * m : SUB * m + SUB, lanes] = reach * wide(weights[m : m + 1, lanes])

    each_tile(rate_ref.shape[1], body)
    tables = ((near_ref, near_far), (reach_ref, reach_far), (power_ref, power_far))
    going = [pltpu.make_async_copy(*pair, sems.at[len(pairs) + i]) for i, pair in enumerate(tables)]
    for each in going:
        each.start()
    near_head[...] = near_ref[:, :width]
    reach_head[...] = reach_ref[:, :width]
    power_head[...] = power_ref[:, :width]
    for each in coming[3:] + going:
        each.wait()


def output_kernel(
    near_ref, lead_ref, reach_ref, power_ref, key_ref, value_ref, received_ref,
    grad_key_ref, grad_value_ref,
    slabs, mixes,
):
    def body(tile, slot):
        lanes = lane_slice(tile)
        slab, mix_sub = slabs.at[slot], mixes.at[slot]
        slab[...] = received_ref[slab_rows(tile, near_ref.shape[1] // LANES), :].astype(F32)
        one = [wide(power_ref[m : m + 1, lanes]) for m in range(MODES)]
        state = []
        for m in range(MODES):
            row = SUB * (QUADS - 1 - m // 4) + m % 4
            rows = slice(SUB * m, SUB * m + SUB)
            state.append(lead_ref[rows, lanes] + wide(slab[row : row + 1, :]) * reach_ref[rows, lanes])
        for j in range(ROWS - 1, -1, -1):
            rows = slice(SUB * j, SUB * j + SUB)
            mix_sub[rows, :] = near_ref[rows, lanes] + halves_sum(state)
            if j > 0:
                state = [s * a for s, a in zip(state, one)]
        for i in range(0, ROWS, 2):
            rows = slice(SUB * i, SUB * i + 16)
            mix = jnp.concatenate([natural(mix_sub, i), natural(mix_sub, i + 1)], axis=0).astype(BF16).astype(F32)
            grad_key_ref[rows, lanes] = (mix * value_ref[rows, lanes].astype(F32)).astype(BF16)
            grad_value_ref[rows, lanes] = (mix * key_ref[rows, lanes].astype(F32)).astype(BF16)

    each_tile(near_ref.shape[1], body, 8)


def gate_kernel(grad_ref, conv_ref, out_ref):
    def body(tile, slot):
        lanes = lane_slice(tile)
        out_ref[:, lanes] = (grad_ref[:, lanes].astype(F32) * conv_ref[:, lanes].astype(F32)).astype(BF16)

    each_tile(grad_ref.shape[1], body)


def streamed(body, ins, outs, width, scratch, flops, moved, heads=(), ahead=3):
    arrays = [x for x, _ in ins + outs]
    n_in, n_all = len(ins), len(ins) + len(outs)
    stays = [kept for _, kept in ins + outs]
    steps = max(x.shape[1] for x in arrays) // width
    moving = [i for i in range(n_all) if not stays[i]]
    first = 1 if heads else 0

    def block(ref, at):
        if ref.shape[1] == LANES:
            size = width // LANES * 32
            return ref.at[pl.ds(pl.multiple_of((steps - 1 - at) * size, size), size), :]
        return ref.at[:, pl.ds(pl.multiple_of(at * width, width), width)]

    def kernel(*refs):
        ready = refs[n_in : n_in + len(heads)]
        refs = refs[:n_in] + refs[n_in + len(heads) :]
        places = dict(zip(moving, refs[n_all : n_all + len(moving)]))
        sems, *extra = refs[n_all + len(moving) :]

        def copy(i, at):
            ends = (block(refs[i], at), block(places[i], at))
            return pltpu.make_async_copy(*(ends if i < n_in else ends[::-1]), sems.at[i, at])

        coming = [i for i in moving if i < n_in]
        going = [i for i in moving if i >= n_in]
        for at in range(first, min(first + ahead, steps)):
            for i in coming:
                copy(i, at).start()

        def work(at, held):
            body(*(held.get(i, block(places.get(i, refs[i]), at)) for i in range(n_all)), *extra)
            for i in going:
                copy(i, at).start()

        def step(at, _):
            @pl.when(at + ahead < steps)
            def _():
                for i in coming:
                    copy(i, at + ahead).start()

            for i in coming:
                copy(i, at).wait()
            work(at, {})
            return 0

        if heads:
            work(0, dict(zip(coming, ready)))
        lax.fori_loop(first, steps, step, 0)
        for at in range(steps):
            for i in going:
                copy(i, at).wait()

    space = [pltpu.VMEM if kept else pltpu.HBM for kept in stays]
    specs = [pl.BlockSpec(memory_space=kind) for kind in space]
    held = [pltpu.with_memory_space_constraint(x, kind) for x, kind in zip(arrays[:n_in], space)]
    held += [pltpu.with_memory_space_constraint(x, pltpu.VMEM) for x in heads]
    results = [kind(x.shape, x.dtype) for x, kind in zip(arrays[n_in:], space[n_in:])]
    return call(
        kernel, (), specs[:n_in] + [pl.BlockSpec(memory_space=pltpu.VMEM)] * len(heads), specs[n_in:], results,
        [pltpu.VMEM(arrays[i].shape, arrays[i].dtype) for i in moving]
        + [pltpu.SemaphoreType.DMA((n_all, steps))]
        + scratch,
        flops, moved, STREAM_LIMIT,
    )(*held)


def call(kernel, grid, in_specs, out_specs, out_shape, scratch=(), flops=10**6, moved=2**20, limit=VMEM_LIMIT):
    return pl.pallas_call(
        kernel,
        grid=grid,
        in_specs=in_specs,
        out_specs=out_specs,
        out_shape=out_shape,
        scratch_shapes=scratch,
        compiler_params=pltpu.CompilerParams(vmem_limit_bytes=limit),
        cost_estimate=pl.CostEstimate(flops=flops, bytes_accessed=moved, transcendentals=0),
    )


def local(query_rows, key_rows, value_rows, conv_rows, grad_rows, residues, decay_rates):
    blocks = lax.axis_size("ctx")
    tokens, channels = query_rows.shape[1:]
    own = channels // blocks
    scale = 1.0 / math.sqrt(blocks * tokens)
    query, key, value, conv, grad = (x[0] for x in (query_rows, key_rows, value_rows, conv_rows, grad_rows))
    rates, residue = decay_rates.T, residues.T

    def table(*shape):
        return pltpu.VMEM(shape, F32)

    token_block = pl.BlockSpec((tokens, WIDTH), lambda n: (0, n))
    mode_block = pl.BlockSpec((MODES, WIDTH), lambda n: (0, n))
    slab_block = pl.BlockSpec((WIDTH // LANES * 32, LANES), lambda n: (channels // WIDTH - 1 - n, 0))
    token_half = jax.ShapeDtypeStruct((tokens, channels), BF16)
    token_full = jax.ShapeDtypeStruct((tokens, channels), F32)
    slabs = jax.ShapeDtypeStruct((blocks * SUB, LANES), BF16)
    steps = (channels // WIDTH,)

    mixed, product, states, entries, summary = call(
        summary_kernel, steps,
        [token_block] * 4 + [mode_block],
        [token_block] * 4 + [slab_block],
        [token_half, token_half, token_full, token_full, slabs],
        [table(4, MODES, WIDTH), table(2, 2, SUB * PITCH, LANES)],
        10**9, 10 * 2**20,
    )(grad, query, key, value, rates)

    def exchange(rows):
        pieces = rows.reshape(blocks, SUB, LANES)
        backwards = [list(range(blocks - 1, -1, -1))]
        moved = lax.all_to_all(pieces, "ctx", split_axis=0, concat_axis=0, axis_index_groups=backwards, tiled=True)
        return moved.reshape(blocks * SUB, LANES)

    received = exchange(summary)

    lead, coef_slabs = streamed(
        functools.partial(local_kernel, scale),
        [(x, False) for x in (mixed, product, states, entries, rates, residue)],
        [(token_full, False), (slabs, True)],
        WIDTH,
        [
            table(MODES, WIDTH), table(MODES, WIDTH), table(2, MODES, WIDTH),
            table(8, 32, LANES), table(3, MODES, WIDTH),
        ],
        10**9, 10 * 2**20,
    )

    me = lax.axis_index("ctx")
    rates_late, _ = lax.optimization_barrier((rates, summary))
    rate_own = lax.dynamic_slice(rates_late, (4 * (me % QUADS), LANES * (me // QUADS)), (4, LANES))
    rate_own = jnp.concatenate([rate_own, rate_own], axis=0)

    vmem = pl.BlockSpec(memory_space=pltpu.VMEM)
    carries = call(
        functools.partial(scan_kernel, scale), (), [vmem] * 3, vmem, slabs, limit=SMALL_LIMIT
    )(received, coef_slabs, rate_own)

    returned = exchange(carries)

    gate_in, key_late, value_late, mixed_late, _ = lax.optimization_barrier((conv, key, value, mixed, carries))
    far_spec, near_spec = pl.BlockSpec(memory_space=pltpu.HBM), pl.BlockSpec(memory_space=pltpu.VMEM)
    head_types = [pltpu.VMEM((x.shape[0], WIDTH), x.dtype) for x in (lead, lead, lead, rates, key, value)]
    near, reach, power, *heads = call(
        stage_kernel, (), [far_spec] * 6, [far_spec] * 3 + [near_spec] * 6,
        [pltpu.HBM(x.shape, F32) for x in (lead, lead, rates)] + head_types,
        [pltpu.VMEM(mixed.shape, BF16)]
        + [pltpu.VMEM(x.shape, F32) for x in (rates, rates, lead, lead, rates, rates, rates)]
        + [pltpu.SemaphoreType.DMA((9,))],
        10**9, 4 * 2**20, STREAM_LIMIT,
    )(*(
        pltpu.with_memory_space_constraint(x, pltpu.HBM)
        for x in (mixed_late, rates, residue, lead, key_late, value_late)
    ))
    grad_query = streamed(
        gate_kernel, [(grad, False), (gate_in, False)], [(token_half, False)], WIDTH, [], 10**6, 3 * 2**20
    )[0]

    coef_part = call(
        total_kernel, (), [vmem], vmem, jax.ShapeDtypeStruct((MODES, own), F32), limit=SMALL_LIMIT
    )(returned)
    other = lax.ppermute(coef_part, "dp", [(0, 1), (1, 0)])

    grad_key, grad_value = streamed(
        output_kernel,
        [(x, False) for x in (near, lead, reach, power, key, value)] + [(returned, True)],
        [(token_half, False), (token_half, False)],
        WIDTH,
        [table(8, 32, LANES), table(8, TOKENS, LANES)],
        10**9, 9 * 2**20, heads,
    )

    coef = (coef_part + other).T
    return (grad_query[None], grad_key[None], grad_value[None], coef)


def solution(mesh):
    rows = P("dp", "ctx", None)
    return jax.shard_map(
        local,
        mesh=mesh,
        in_specs=(rows, rows, rows, rows, rows, P(), P()),
        out_specs=(rows, rows, rows, P("ctx", None)),
        check_vma=False,
    )
```

```python
import functools
import math

import jax
import jax.numpy as jnp
from jax import lax
from jax.experimental import pallas as pl
from jax.experimental.pallas import tpu as pltpu
from jax.sharding import PartitionSpec as P

F32 = jnp.float32
BF16 = jnp.bfloat16
LANES = 128
SUB = 8
TOKENS = 128
ROWS = TOKENS // SUB
MODES = 16
QUADS = 4
PITCH = 24
WIDTH = 1024
VMEM_LIMIT = 60 * 1024 * 1024
SMALL_LIMIT = 4 * 1024 * 1024
STREAM_LIMIT = 40 * 1024 * 1024


def lane_slice(tile):
    return pl.ds(pl.multiple_of(tile * LANES, LANES), LANES)


def slab_rows(tile, tiles):
    return pl.ds(pl.multiple_of((tiles - 1 - tile) * 32, 32), 32)


def gain_of(rates):
    square = rates * rates
    series = 1.0 + square * (1.0 / 6.0 + square * (1.0 / 120.0 + square * (1.0 / 5040.0)))
    return jnp.sqrt(2.0 * rates * series * jnp.exp(-rates))


def wide(row):
    return jnp.broadcast_to(row, (SUB, LANES))


def halves_sum(terms):
    while len(terms) > 1:
        terms = [x + y for x, y in zip(terms[::2], terms[1::2])]
    return terms[0]


def swap_quarters(tile):
    j = lax.broadcasted_iota(jnp.int32, (SUB, LANES), 0) & 3
    q = lax.broadcasted_iota(jnp.int32, (SUB, LANES), 1) >> 5
    for bit in (1, 2):
        j_set = (j & bit) != 0
        q_set = (q & bit) != 0
        up, down = pltpu.roll(tile, bit, 0), pltpu.roll(tile, SUB - bit, 0)
        if bit == 2:
            moved = pltpu.roll(jnp.where(j_set, up, down), 64, 1)
        else:
            moved = jnp.where(j_set, pltpu.roll(up, LANES - 32, 1), pltpu.roll(down, 32, 1))
        tile = jnp.where(j_set == q_set, tile, moved)
    return tile


def natural(tokens_sub, row):
    return tokens_sub[pl.ds(64 * (row % 2) + row // 2, SUB, stride=SUB), :]


def fold(first, second, bit, place):
    clear = (place & bit) == 0
    left = jnp.where(clear, first, pltpu.roll(second, bit, 0))
    right = jnp.where(clear, pltpu.roll(first, SUB - bit, 0), second)
    return left + right


def sublane_sums(tiles, place):
    for bit in (4, 2, 1):
        tiles = [fold(tiles[i], tiles[i + bit], bit, place) for i in range(bit)]
    return tiles[0]


def each_tile(width, body, slots=2):
    def some(at, _):
        for slot in range(slots):
            body(slots * at + slot, slot)
        return 0

    lax.fori_loop(0, width // (slots * LANES), some, 0)


def weighted_sums(state, entry, rows_of, place):
    for bit, power in ((4, 3), (2, 2), (1, 1)):
        clear = (place & bit) == 0
        weights = [rows_of(power, bit, i) for i in range(bit)]
        for which, tiles in enumerate((state, entry)):
            folded = []
            for i, weight in enumerate(weights):
                first, second = tiles[i], tiles[i + bit]
                left = jnp.where(clear, first, pltpu.roll(second, bit, 0))
                right = jnp.where(clear, pltpu.roll(first, SUB - bit, 0), second)
                folded.append(left + weight * right if which == 0 else right + weight * left)
            if which == 0:
                state = folded
            else:
                entry = folded
    return state[0], entry[0]


def summary_kernel(
    grad_ref, query_ref, key_ref, value_ref, rate_ref,
    mixed_ref, product_ref, state_ref, entry_ref, send_ref, own_ref,
    powers, full,
):
    rates = rate_ref[...]
    for index, power in enumerate((1.0, 16.0, 32.0, 64.0)):
        powers[index] = jnp.exp(-power * rates)
    place = lax.broadcasted_iota(jnp.int32, (SUB, LANES), 0)
    low = place < 4
    tiles = grad_ref.shape[1] // LANES
    me = lax.axis_index("ctx")
    tile_own, quad = me // QUADS, me % QUADS

    @pl.when(pl.program_id(0) == tile_own // tiles)
    def _():
        lanes = lane_slice(tile_own % tiles)
        eight = jnp.where(quad >= 2, rate_ref[SUB:, lanes], rate_ref[:SUB, lanes])
        turned = pltpu.roll(eight, 4, 0)
        own_ref[...] = jnp.where(low == (quad % 2 == 0), eight, turned)

    def body(tile, slot):
        lanes = lane_slice(tile)
        mixed_full, product_full = full.at[slot, 0], full.at[slot, 1]
        mixed = (grad_ref[:, lanes].astype(F32) * query_ref[:, lanes].astype(F32)).astype(BF16)
        product = (key_ref[:, lanes].astype(F32) * value_ref[:, lanes].astype(F32)).astype(BF16)
        mixed, product = mixed.astype(F32), product.astype(F32)
        for i in range(ROWS):
            at, rows = PITCH * (i // 2) + SUB * (i % 2), slice(SUB * i, SUB * i + SUB)
            mixed_full[at : at + SUB, :] = mixed[rows, :]
            product_full[at : at + SUB, :] = product[rows, :]
        g = [mixed_full[pl.ds(j, SUB, stride=PITCH), :] for j in range(ROWS)]
        p = [product_full[pl.ds(j, SUB, stride=PITCH), :] for j in range(ROWS)]
        for j in range(0, ROWS, 2):
            rows = slice(SUB * j, SUB * j + 16)
            mixed_ref[rows, lanes] = jnp.concatenate([g[j], g[j + 1]], axis=0).astype(BF16)
            product_ref[rows, lanes] = jnp.concatenate([p[j], p[j + 1]], axis=0).astype(BF16)
        sums = []
        for half in range(2):
            states, entries = [], []
            for base in range(SUB * half, SUB * half + SUB, 4):
                group = range(base, base + 4)
                one = [wide(powers[0, m : m + 1, lanes]) for m in group]
                state = [g[ROWS - 1]] * 4
                entry = [p[0] * a for a in one]
                for i in range(1, ROWS):
                    state = [s * a + g[ROWS - 1 - i] for s, a in zip(state, one)]
                    entry = [(e + p[i]) * a for e, a in zip(entry, one)]
                for s, e, m in zip(state, entry, group):
                    state_ref[SUB * m : SUB * m + SUB, lanes] = s
                    entry_ref[SUB * m : SUB * m + SUB, lanes] = e
                states += state
                entries += entry

            def rows_of(power, bit, i):
                if bit == 1:
                    return powers[power, SUB * half : SUB * half + SUB, lanes]
                modes = [SUB * half + i + bit * at for at in range(SUB // bit)]
                out = wide(powers[power, modes[-1] : modes[-1] + 1, lanes])
                for at in range(len(modes) - 2, -1, -1):
                    out = jnp.where(place < bit * (at + 1), wide(powers[power, modes[at] : modes[at] + 1, lanes]), out)
                return out

            s, e = weighted_sums(states, entries, rows_of, place)
            sums += [jnp.where(low, s, pltpu.roll(e, 4, 0)), jnp.where(low, pltpu.roll(s, 4, 0), e)]
        rows = slab_rows(tile, grad_ref.shape[1] // LANES)
        send_ref[rows, :] = jnp.concatenate(sums[::-1], axis=0).astype(BF16)

    each_tile(grad_ref.shape[1], body)


def local_kernel(
    scale, mixed_ref, product_ref, state_ref, entry_ref, rate_ref, residue_ref,
    lead_ref, send_ref,
    powers, weights, lags, slabs, runs,
):
    rates = rate_ref[...]
    powers[...] = jnp.exp(-rates)
    gains = gain_of(rates)
    weights[...] = residue_ref[...] * gains * powers[...]
    for index, power in enumerate((16.0, 32.0, 64.0)):
        runs[index] = jnp.exp(-power * rates)
    place = lax.broadcasted_iota(jnp.int32, (SUB, LANES), 0)

    def body(tile, slot):
        lanes = lane_slice(tile)
        g, p = [], []
        for j in range(0, ROWS, 2):
            rows = slice(SUB * j, SUB * j + 16)
            pair = mixed_ref[rows, lanes].astype(F32)
            g += [pair[:SUB, :], pair[SUB:, :]]
            pair = product_ref[rows, lanes].astype(F32)
            p += [pair[:SUB, :], pair[SUB:, :]]
        lag = []
        for d in range(ROWS):
            total = g[d] * p[0]
            for j in range(1, ROWS - d):
                total = total + g[j + d] * p[j]
            lag.append(total)
        for half in range(2):
            rows = slice(SUB * half, SUB * half + SUB)
            lags[0, rows, lanes] = sublane_sums(lag[rows], place)
            cross = []
            for m in range(SUB * half, SUB * half + SUB):
                mode_rows = slice(SUB * m, SUB * m + SUB)
                carry = state_ref[mode_rows, lanes]
                for index, step in ((0, 1), (1, 2), (2, 4)):
                    later = jnp.where(place < SUB - step, pltpu.roll(carry, SUB - step, 0), 0.0)
                    carry = carry + wide(runs[index, m : m + 1, lanes]) * later
                carry = jnp.where(place < SUB - 1, pltpu.roll(carry, SUB - 1, 0), 0.0)
                cross.append(carry * entry_ref[mode_rows, lanes])
                lead_ref[mode_rows, lanes] = carry * wide(weights[m : m + 1, lanes])
            lags[1, rows, lanes] = sublane_sums(cross, place)

    each_tile(mixed_ref.shape[1], body)
    coef = jnp.broadcast_to(lags[0, ROWS - 1 : ROWS, :], rates.shape)
    for d in range(ROWS - 2, -1, -1):
        coef = coef * powers[...] + lags[0, d : d + 1, :]
    lags[1] = (coef + lags[1]) * gains * scale
    slabs[...] = jnp.zeros_like(slabs)

    def ship(tile, slot):
        lanes = lane_slice(tile)
        slab = slabs.at[slot]
        for pair in range(2):
            moved = swap_quarters(lags[1, SUB * pair : SUB * pair + SUB, lanes])
            for k in range(2):
                for q in range(4):
                    row = SUB * (QUADS - 1 - q) + 4 + 2 * pair + k
                    slab[row : row + 1, :] = moved[4 * k + q : 4 * k + q + 1, :]
        send_ref[slab_rows(tile, mixed_ref.shape[1] // LANES), :] = slab[...].astype(BF16)

    each_tile(mixed_ref.shape[1], ship, 8)


def scan_kernel(scale, received_ref, coef_ref, rate_ref, send_ref):
    blocks = received_ref.shape[0] // SUB
    rates = rate_ref[...]
    decay = jnp.exp(-float(TOKENS) * rates)
    place = lax.broadcasted_iota(jnp.int32, (SUB, LANES), 0)
    low = place < 4

    squared = decay * decay
    gains = gain_of(rates) * scale

    def step(back, held):
        state, far, far_even = held
        start = pl.multiple_of(back * 16, 16)
        pair = received_ref[pl.ds(start, 16), :].astype(F32)
        coef = coef_ref[pl.ds(start, 16), :].astype(F32)
        odd, even = pair[:SUB, :], pair[SUB:, :]
        odd_own = jnp.where(low, odd, pltpu.roll(odd, 4, 0))
        even_own = jnp.where(low, even, pltpu.roll(even, 4, 0))
        before = odd_own + decay * state
        out = [jnp.where(low, state, coef[:SUB, :]), jnp.where(low, before, coef[SUB:, :])]
        send_ref[pl.ds(start, 16), :] = jnp.concatenate(out, axis=0).astype(BF16)
        return (even_own + decay * odd_own) + squared * state, far + odd * state, far_even + even * before

    zero = jnp.zeros((SUB, LANES), F32)
    _, far, far_even = lax.fori_loop(0, blocks // 2, step, (zero, zero, zero), unroll=8)
    far = swap_quarters((far + far_even) * gains)
    me = lax.axis_index("ctx")
    mine = slab_rows(me // QUADS, blocks // QUADS)
    extra = [jnp.where(place == 4 + me % QUADS, wide(far[4 + q : 5 + q, :]), 0.0) for q in range(QUADS - 1, -1, -1)]
    send_ref[mine, :] = (send_ref[mine, :].astype(F32) + jnp.concatenate(extra, axis=0)).astype(BF16)


def total_kernel(received_ref, out_ref):
    def step(at, held):
        rows = received_ref[pl.ds(pl.multiple_of(at * 16, 16), 16), :].astype(F32)
        return held[0] + rows[:SUB, :], held[1] + rows[SUB:, :]

    zero = jnp.zeros((SUB, LANES), F32)
    first, second = lax.fori_loop(0, received_ref.shape[0] // 16, step, (zero, zero), unroll=8)
    total = first + second
    width = out_ref.shape[1]
    for k in range(QUADS):
        for j in range(4):
            out_ref[4 * k + j : 4 * k + j + 1, :] = total[4 + k : 5 + k, width * j : width * j + width]


def stage_kernel(
    mixed_far, rate_far, residue_far, lead_far, key_far, value_far, grad_far, conv_far,
    near_far, reach_far, power_far, gate_far, near_head, lead_head, reach_head, power_head, key_head, value_head,
    mixed_ref, rate_ref, residue_ref, near_ref, reach_ref, power_ref, grad_ref, conv_ref, gate_ref, weights, taps, sems,
):
    width = near_head.shape[1]
    steps = mixed_ref.shape[1] // width
    heads = ((lead_far, lead_head), (key_far, key_head), (value_far, value_head))
    pairs = [(rate_far, rate_ref), (residue_far, residue_ref), (mixed_far, mixed_ref), (grad_far, grad_ref), (conv_far, conv_ref)]
    pairs += [(far.at[:, pl.ds(0, width)], head) for far, head in heads]
    coming = [pltpu.make_async_copy(*pair, sems.at[i, 0]) for i, pair in enumerate(pairs)]
    for each in coming:
        each.start()
    for each in coming[:2]:
        each.wait()
    power_ref[...] = jnp.exp(-rate_ref[...])
    term = residue_ref[...] * gain_of(rate_ref[...])
    for d in range(ROWS):
        taps[d : d + 1, :] = jnp.sum(term, axis=0, keepdims=True)
        term = term * power_ref[...]
        if d == 0:
            weights[...] = term
    back = (16 * (SUB - 1 - lax.broadcasted_iota(jnp.int32, (SUB, LANES), 0))).astype(F32)
    for each in coming[2:5]:
        each.wait()

    def out_copy(i, at):
        source, target = ((near_ref, near_far), (reach_ref, reach_far), (power_ref, power_far), (gate_ref, gate_far))[i]
        lanes = pl.ds(pl.multiple_of(at * width, width), width)
        return pltpu.make_async_copy(source.at[:, lanes], target.at[:, lanes], sems.at[len(pairs) + i, at])

    def body(tile, slot):
        lanes = lane_slice(tile)
        gate_ref[:, lanes] = (grad_ref[:, lanes].astype(F32) * conv_ref[:, lanes].astype(F32)).astype(BF16)
        g = []
        for j in range(0, ROWS, 2):
            pair = mixed_ref[SUB * j : SUB * j + 16, lanes].astype(F32)
            g += [pair[:SUB, :], pair[SUB:, :]]
        near = [None] * ROWS
        for d in range(ROWS):
            tap = wide(taps[d : d + 1, lanes])
            for j in range(ROWS - d):
                near[j] = tap * g[j + d] if d == 0 else near[j] + tap * g[j + d]
        for j in range(ROWS):
            near_ref[SUB * j : SUB * j + SUB, lanes] = near[j]
        for m in range(MODES):
            reach = jnp.exp(-back * wide(rate_ref[m : m + 1, lanes]))
            reach_ref[SUB * m : SUB * m + SUB, lanes] = reach * wide(weights[m : m + 1, lanes])

    def step(at, _):
        each_tile(width, lambda tile, slot: body(tile + at * (width // LANES), slot))
        for i in range(4):
            out_copy(i, at).start()
        return 0

    lax.fori_loop(0, steps, step, 0)
    near_head[...] = near_ref[:, :width]
    reach_head[...] = reach_ref[:, :width]
    power_head[...] = power_ref[:, :width]
    for each in coming[5:]:
        each.wait()
    for at in range(steps):
        for i in range(4):
            out_copy(i, at).wait()


def output_kernel(
    near_ref, lead_ref, reach_ref, power_ref, key_ref, value_ref, received_ref,
    grad_key_ref, grad_value_ref,
    slabs, mixes,
):
    def body(tile, slot):
        lanes = lane_slice(tile)
        slab, mix_sub = slabs.at[slot], mixes.at[slot]
        slab[...] = received_ref[slab_rows(tile, near_ref.shape[1] // LANES), :].astype(F32)
        one = [wide(power_ref[m : m + 1, lanes]) for m in range(MODES)]
        state = []
        for m in range(MODES):
            row = SUB * (QUADS - 1 - m // 4) + m % 4
            rows = slice(SUB * m, SUB * m + SUB)
            state.append(lead_ref[rows, lanes] + wide(slab[row : row + 1, :]) * reach_ref[rows, lanes])
        for j in range(ROWS - 1, -1, -1):
            rows = slice(SUB * j, SUB * j + SUB)
            mix_sub[rows, :] = near_ref[rows, lanes] + halves_sum(state)
            if j > 0:
                state = [s * a for s, a in zip(state, one)]
        for i in range(0, ROWS, 2):
            rows = slice(SUB * i, SUB * i + 16)
            mix = jnp.concatenate([natural(mix_sub, i), natural(mix_sub, i + 1)], axis=0).astype(BF16).astype(F32)
            grad_key_ref[rows, lanes] = (mix * value_ref[rows, lanes].astype(F32)).astype(BF16)
            grad_value_ref[rows, lanes] = (mix * key_ref[rows, lanes].astype(F32)).astype(BF16)

    each_tile(near_ref.shape[1], body, 8)


def streamed(body, ins, outs, width, scratch, flops, moved, heads=(), ahead=3):
    arrays = [x for x, _ in ins + outs]
    n_in, n_all = len(ins), len(ins) + len(outs)
    stays = [kept for _, kept in ins + outs]
    steps = max(x.shape[1] for x in arrays) // width
    moving = [i for i in range(n_all) if not stays[i]]
    first = 1 if heads else 0

    def block(ref, at):
        if ref.shape[1] == LANES:
            size = width // LANES * 32
            return ref.at[pl.ds(pl.multiple_of((steps - 1 - at) * size, size), size), :]
        return ref.at[:, pl.ds(pl.multiple_of(at * width, width), width)]

    def kernel(*refs):
        ready = refs[n_in : n_in + len(heads)]
        refs = refs[:n_in] + refs[n_in + len(heads) :]
        places = dict(zip(moving, refs[n_all : n_all + len(moving)]))
        sems, *extra = refs[n_all + len(moving) :]

        def copy(i, at):
            ends = (block(refs[i], at), block(places[i], at))
            return pltpu.make_async_copy(*(ends if i < n_in else ends[::-1]), sems.at[i, at])

        coming = [i for i in moving if i < n_in]
        going = [i for i in moving if i >= n_in]
        for at in range(first, min(first + ahead, steps)):
            for i in coming:
                copy(i, at).start()

        def work(at, held):
            body(*(held.get(i, block(places.get(i, refs[i]), at)) for i in range(n_all)), *extra)
            for i in going:
                copy(i, at).start()

        def step(at, _):
            @pl.when(at + ahead < steps)
            def _():
                for i in coming:
                    copy(i, at + ahead).start()

            for i in coming:
                copy(i, at).wait()
            work(at, {})
            return 0

        if heads:
            work(0, dict(zip(coming, ready)))
        lax.fori_loop(first, steps, step, 0)
        for at in range(steps):
            for i in going:
                copy(i, at).wait()

    space = [pltpu.VMEM if kept else pltpu.HBM for kept in stays]
    specs = [pl.BlockSpec(memory_space=kind) for kind in space]
    held = [pltpu.with_memory_space_constraint(x, kind) for x, kind in zip(arrays[:n_in], space)]
    held += [pltpu.with_memory_space_constraint(x, pltpu.VMEM) for x in heads]
    results = [kind(x.shape, x.dtype) for x, kind in zip(arrays[n_in:], space[n_in:])]
    return call(
        kernel, (), specs[:n_in] + [pl.BlockSpec(memory_space=pltpu.VMEM)] * len(heads), specs[n_in:], results,
        [pltpu.VMEM(arrays[i].shape, arrays[i].dtype) for i in moving]
        + [pltpu.SemaphoreType.DMA((n_all, steps))]
        + scratch,
        flops, moved, STREAM_LIMIT,
    )(*held)


def call(kernel, grid, in_specs, out_specs, out_shape, scratch=(), flops=10**6, moved=2**20, limit=VMEM_LIMIT):
    return pl.pallas_call(
        kernel,
        grid=grid,
        in_specs=in_specs,
        out_specs=out_specs,
        out_shape=out_shape,
        scratch_shapes=scratch,
        compiler_params=pltpu.CompilerParams(vmem_limit_bytes=limit),
        cost_estimate=pl.CostEstimate(flops=flops, bytes_accessed=moved, transcendentals=0),
    )


def local(query_rows, key_rows, value_rows, conv_rows, grad_rows, residues, decay_rates):
    blocks = lax.axis_size("ctx")
    tokens, channels = query_rows.shape[1:]
    own = channels // blocks
    scale = 1.0 / math.sqrt(blocks * tokens)
    query, key, value, conv, grad = (x[0] for x in (query_rows, key_rows, value_rows, conv_rows, grad_rows))
    rates, residue = decay_rates.T, residues.T

    def table(*shape):
        return pltpu.VMEM(shape, F32)

    token_block = pl.BlockSpec((tokens, WIDTH), lambda n: (0, n))
    mode_block = pl.BlockSpec((MODES, WIDTH), lambda n: (0, n))
    slab_block = pl.BlockSpec((WIDTH // LANES * 32, LANES), lambda n: (channels // WIDTH - 1 - n, 0))
    token_half = jax.ShapeDtypeStruct((tokens, channels), BF16)
    token_full = jax.ShapeDtypeStruct((tokens, channels), F32)
    slabs = jax.ShapeDtypeStruct((blocks * SUB, LANES), BF16)
    steps = (channels // WIDTH,)

    mixed, product, states, entries, summary, rate_own = call(
        summary_kernel, steps,
        [token_block] * 4 + [mode_block],
        [token_block] * 4 + [slab_block, pl.BlockSpec((SUB, LANES), lambda n: (0, 0))],
        [token_half, token_half, token_full, token_full, slabs, jax.ShapeDtypeStruct((SUB, LANES), F32)],
        [table(4, MODES, WIDTH), table(2, 2, SUB * PITCH, LANES)],
        10**9, 10 * 2**20,
    )(grad, query, key, value, rates)

    def exchange(rows):
        pieces = rows.reshape(blocks, SUB, LANES)
        backwards = [list(range(blocks - 1, -1, -1))]
        moved = lax.all_to_all(pieces, "ctx", split_axis=0, concat_axis=0, axis_index_groups=backwards, tiled=True)
        return moved.reshape(blocks * SUB, LANES)

    received = exchange(summary)

    lead, coef_slabs = streamed(
        functools.partial(local_kernel, scale),
        [(x, False) for x in (mixed, product, states, entries, rates, residue)],
        [(token_full, False), (slabs, True)],
        WIDTH,
        [
            table(MODES, WIDTH), table(MODES, WIDTH), table(2, MODES, WIDTH),
            table(8, 32, LANES), table(3, MODES, WIDTH),
        ],
        10**9, 10 * 2**20,
    )

    vmem = pl.BlockSpec(memory_space=pltpu.VMEM)
    carries = call(
        functools.partial(scan_kernel, scale), (), [vmem] * 3, vmem, slabs, limit=SMALL_LIMIT
    )(received, coef_slabs, rate_own)

    returned = exchange(carries)

    conv_late, key_late, value_late, mixed_late, grad_late, _ = lax.optimization_barrier(
        (conv, key, value, mixed, grad, carries)
    )
    far_spec, near_spec = pl.BlockSpec(memory_space=pltpu.HBM), pl.BlockSpec(memory_space=pltpu.VMEM)
    head_types = [pltpu.VMEM((x.shape[0], WIDTH), x.dtype) for x in (lead, lead, lead, rates, key, value)]
    near, reach, power, grad_query, *heads = call(
        stage_kernel, (), [far_spec] * 8, [far_spec] * 4 + [near_spec] * 6,
        [pltpu.HBM(x.shape, x.dtype) for x in (lead, lead, rates, key)] + head_types,
        [pltpu.VMEM(mixed.shape, BF16)]
        + [pltpu.VMEM(x.shape, F32) for x in (rates, rates, lead, lead, rates)]
        + [pltpu.VMEM(mixed.shape, BF16)] * 3
        + [pltpu.VMEM(x.shape, F32) for x in (rates, rates)]
        + [pltpu.SemaphoreType.DMA((12, steps[0]))],
        10**9, 8 * 2**20, STREAM_LIMIT,
    )(*(
        pltpu.with_memory_space_constraint(x, pltpu.HBM)
        for x in (mixed_late, rates, residue, lead, key_late, value_late, grad_late, conv_late)
    ))

    coef_part = call(
        total_kernel, (), [vmem], vmem, jax.ShapeDtypeStruct((MODES, own), F32), limit=SMALL_LIMIT
    )(returned)
    other = lax.ppermute(coef_part, "dp", [(0, 1), (1, 0)])

    grad_key, grad_value = streamed(
        output_kernel,
        [(x, False) for x in (near, lead, reach, power, key, value)] + [(returned, True)],
        [(token_half, False), (token_half, False)],
        WIDTH,
        [table(8, 32, LANES), table(8, TOKENS, LANES)],
        10**9, 9 * 2**20, heads,
    )

    coef = (coef_part + other).T
    return (grad_query[None], grad_key[None], grad_value[None], coef)


def solution(mesh):
    rows = P("dp", "ctx", None)
    return jax.shard_map(
        local,
        mesh=mesh,
        in_specs=(rows, rows, rows, rows, rows, P(), P()),
        out_specs=(rows, rows, rows, P("ctx", None)),
        check_vma=False,
    )
```

```python
import functools
import math

import jax
import jax.numpy as jnp
from jax import lax
from jax.experimental import pallas as pl
from jax.experimental.pallas import tpu as pltpu
from jax.sharding import PartitionSpec as P

F32 = jnp.float32
BF16 = jnp.bfloat16
LANES = 128
SUB = 8
TOKENS = 128
ROWS = TOKENS // SUB
MODES = 16
QUADS = 4
PITCH = 24
FIRST = 107
WIDTH = 1024
VMEM_LIMIT = 60 * 1024 * 1024
SMALL_LIMIT = 4 * 1024 * 1024
STREAM_LIMIT = 40 * 1024 * 1024


def lane_slice(tile):
    return pl.ds(pl.multiple_of(tile * LANES, LANES), LANES)


def slab_rows(tile, tiles):
    return pl.ds(pl.multiple_of((tile ^ ((FIRST >> 2) & (tiles - 1))) * 32, 32), 32)


def gain_of(rates):
    square = rates * rates
    series = 1.0 + square * (1.0 / 6.0 + square * (1.0 / 120.0 + square * (1.0 / 5040.0)))
    return jnp.sqrt(2.0 * rates * series * jnp.exp(-rates))


def wide(row):
    return jnp.broadcast_to(row, (SUB, LANES))


def halves_sum(terms):
    while len(terms) > 1:
        terms = [x + y for x, y in zip(terms[::2], terms[1::2])]
    return terms[0]


def swap_quarters(tile):
    j = lax.broadcasted_iota(jnp.int32, (SUB, LANES), 0) & 3
    q = lax.broadcasted_iota(jnp.int32, (SUB, LANES), 1) >> 5
    for bit in (1, 2):
        j_set = (j & bit) != 0
        q_set = (q & bit) != 0
        up, down = pltpu.roll(tile, bit, 0), pltpu.roll(tile, SUB - bit, 0)
        if bit == 2:
            moved = pltpu.roll(jnp.where(j_set, up, down), 64, 1)
        else:
            moved = jnp.where(j_set, pltpu.roll(up, LANES - 32, 1), pltpu.roll(down, 32, 1))
        tile = jnp.where(j_set == q_set, tile, moved)
    return tile


def natural(tokens_sub, row):
    return tokens_sub[pl.ds(64 * (row % 2) + row // 2, SUB, stride=SUB), :]


def fold(first, second, bit, place):
    clear = (place & bit) == 0
    left = jnp.where(clear, first, pltpu.roll(second, bit, 0))
    right = jnp.where(clear, pltpu.roll(first, SUB - bit, 0), second)
    return left + right


def sublane_sums(tiles, place):
    for bit in (4, 2, 1):
        tiles = [fold(tiles[i], tiles[i + bit], bit, place) for i in range(bit)]
    return tiles[0]


def each_tile(width, body, slots=2):
    def some(at, _):
        for slot in range(slots):
            body(slots * at + slot, slot)
        return 0

    lax.fori_loop(0, width // (slots * LANES), some, 0)


def weighted_sums(state, entry, rows_of, place):
    for bit, power in ((4, 3), (2, 2), (1, 1)):
        clear = (place & bit) == 0
        weights = [rows_of(power, bit, i) for i in range(bit)]
        for which, tiles in enumerate((state, entry)):
            folded = []
            for i, weight in enumerate(weights):
                first, second = tiles[i], tiles[i + bit]
                left = jnp.where(clear, first, pltpu.roll(second, bit, 0))
                right = jnp.where(clear, pltpu.roll(first, SUB - bit, 0), second)
                folded.append(left + weight * right if which == 0 else right + weight * left)
            if which == 0:
                state = folded
            else:
                entry = folded
    return state[0], entry[0]


def summary_kernel(
    grad_ref, query_ref, key_ref, value_ref, rate_ref,
    mixed_ref, product_ref, state_ref, entry_ref, send_ref, own_ref,
    powers, full,
):
    rates = rate_ref[...]
    for index, power in enumerate((1.0, 16.0, 32.0, 64.0)):
        powers[index] = jnp.exp(-power * rates)
    place = lax.broadcasted_iota(jnp.int32, (SUB, LANES), 0)
    low = place < 4
    tiles = grad_ref.shape[1] // LANES
    me = lax.axis_index("ctx")
    tile_own, quad = me // QUADS, me % QUADS

    @pl.when(pl.program_id(0) == tile_own // tiles)
    def _():
        lanes = lane_slice(tile_own % tiles)
        eight = jnp.where(quad >= 2, rate_ref[SUB:, lanes], rate_ref[:SUB, lanes])
        turned = pltpu.roll(eight, 4, 0)
        own_ref[...] = jnp.where(low == (quad % 2 == 0), eight, turned)

    def body(tile, slot):
        lanes = lane_slice(tile)
        mixed_full, product_full = full.at[slot, 0], full.at[slot, 1]
        mixed = (grad_ref[:, lanes].astype(F32) * query_ref[:, lanes].astype(F32)).astype(BF16)
        product = (key_ref[:, lanes].astype(F32) * value_ref[:, lanes].astype(F32)).astype(BF16)
        mixed, product = mixed.astype(F32), product.astype(F32)
        for i in range(ROWS):
            at, rows = PITCH * (i // 2) + SUB * (i % 2), slice(SUB * i, SUB * i + SUB)
            mixed_full[at : at + SUB, :] = mixed[rows, :]
            product_full[at : at + SUB, :] = product[rows, :]
        g = [mixed_full[pl.ds(j, SUB, stride=PITCH), :] for j in range(ROWS)]
        p = [product_full[pl.ds(j, SUB, stride=PITCH), :] for j in range(ROWS)]
        for j in range(0, ROWS, 2):
            rows = slice(SUB * j, SUB * j + 16)
            mixed_ref[rows, lanes] = jnp.concatenate([g[j], g[j + 1]], axis=0).astype(BF16)
            product_ref[rows, lanes] = jnp.concatenate([p[j], p[j + 1]], axis=0).astype(BF16)
        sums = []
        for half in range(2):
            states, entries = [], []
            for base in range(SUB * half, SUB * half + SUB, 4):
                group = range(base, base + 4)
                one = [wide(powers[0, m : m + 1, lanes]) for m in group]
                state = [g[ROWS - 1]] * 4
                entry = [p[0] * a for a in one]
                for i in range(1, ROWS):
                    state = [s * a + g[ROWS - 1 - i] for s, a in zip(state, one)]
                    entry = [(e + p[i]) * a for e, a in zip(entry, one)]
                for s, e, m in zip(state, entry, group):
                    state_ref[SUB * m : SUB * m + SUB, lanes] = s
                    entry_ref[SUB * m : SUB * m + SUB, lanes] = e
                states += state
                entries += entry

            def rows_of(power, bit, i):
                if bit == 1:
                    return powers[power, SUB * half : SUB * half + SUB, lanes]
                modes = [SUB * half + i + bit * at for at in range(SUB // bit)]
                out = wide(powers[power, modes[-1] : modes[-1] + 1, lanes])
                for at in range(len(modes) - 2, -1, -1):
                    out = jnp.where(place < bit * (at + 1), wide(powers[power, modes[at] : modes[at] + 1, lanes]), out)
                return out

            s, e = weighted_sums(states, entries, rows_of, place)
            sums += [jnp.where(low, s, pltpu.roll(e, 4, 0)), jnp.where(low, pltpu.roll(s, 4, 0), e)]
        rows = slab_rows(tile, grad_ref.shape[1] // LANES)
        send_ref[rows, :] = jnp.concatenate(sums[::-1], axis=0).astype(BF16)

    each_tile(grad_ref.shape[1], body)


def local_kernel(
    scale, mixed_ref, product_ref, state_ref, entry_ref, rate_ref, residue_ref,
    lead_ref, send_ref,
    powers, weights, lags, slabs, runs,
):
    rates = rate_ref[...]
    powers[...] = jnp.exp(-rates)
    gains = gain_of(rates)
    weights[...] = residue_ref[...] * gains * powers[...]
    for index, power in enumerate((16.0, 32.0, 64.0)):
        runs[index] = jnp.exp(-power * rates)
    place = lax.broadcasted_iota(jnp.int32, (SUB, LANES), 0)

    def body(tile, slot):
        lanes = lane_slice(tile)
        g, p = [], []
        for j in range(0, ROWS, 2):
            rows = slice(SUB * j, SUB * j + 16)
            pair = mixed_ref[rows, lanes].astype(F32)
            g += [pair[:SUB, :], pair[SUB:, :]]
            pair = product_ref[rows, lanes].astype(F32)
            p += [pair[:SUB, :], pair[SUB:, :]]
        lag = []
        for d in range(ROWS):
            total = g[d] * p[0]
            for j in range(1, ROWS - d):
                total = total + g[j + d] * p[j]
            lag.append(total)
        for half in range(2):
            rows = slice(SUB * half, SUB * half + SUB)
            lags[0, rows, lanes] = sublane_sums(lag[rows], place)
            cross = []
            for m in range(SUB * half, SUB * half + SUB):
                mode_rows = slice(SUB * m, SUB * m + SUB)
                carry = state_ref[mode_rows, lanes]
                for index, step in ((0, 1), (1, 2), (2, 4)):
                    later = jnp.where(place < SUB - step, pltpu.roll(carry, SUB - step, 0), 0.0)
                    carry = carry + wide(runs[index, m : m + 1, lanes]) * later
                carry = jnp.where(place < SUB - 1, pltpu.roll(carry, SUB - 1, 0), 0.0)
                cross.append(carry * entry_ref[mode_rows, lanes])
                lead_ref[mode_rows, lanes] = carry * wide(weights[m : m + 1, lanes])
            lags[1, rows, lanes] = sublane_sums(cross, place)

    each_tile(mixed_ref.shape[1], body)
    coef = jnp.broadcast_to(lags[0, ROWS - 1 : ROWS, :], rates.shape)
    for d in range(ROWS - 2, -1, -1):
        coef = coef * powers[...] + lags[0, d : d + 1, :]
    lags[1] = (coef + lags[1]) * gains * scale
    slabs[...] = jnp.zeros_like(slabs)

    def ship(tile, slot):
        lanes = lane_slice(tile)
        slab = slabs.at[slot]
        for pair in range(2):
            moved = swap_quarters(lags[1, SUB * pair : SUB * pair + SUB, lanes])
            for k in range(2):
                for q in range(4):
                    row = SUB * (QUADS - 1 - q) + 4 + 2 * pair + k
                    slab[row : row + 1, :] = moved[4 * k + q : 4 * k + q + 1, :]
        send_ref[slab_rows(tile, mixed_ref.shape[1] // LANES), :] = slab[...].astype(BF16)

    each_tile(mixed_ref.shape[1], ship, 8)


def scan_kernel(scale, received_ref, coef_ref, rate_ref, send_ref):
    blocks = received_ref.shape[0] // SUB
    rates = rate_ref[...]
    decay = jnp.exp(-float(TOKENS) * rates)
    place = lax.broadcasted_iota(jnp.int32, (SUB, LANES), 0)
    low = place < 4

    squared = decay * decay
    gains = gain_of(rates) * scale

    def step(back, held):
        state, far, far_even = held
        start = pl.multiple_of(((blocks // 2 - 1 - back) ^ (FIRST >> 1)) * 16, 16)
        pair = received_ref[pl.ds(start, 16), :].astype(F32)
        coef = coef_ref[pl.ds(start, 16), :].astype(F32)
        odd, even = pair[:SUB, :], pair[SUB:, :]
        odd_own = jnp.where(low, odd, pltpu.roll(odd, 4, 0))
        even_own = jnp.where(low, even, pltpu.roll(even, 4, 0))
        before = odd_own + decay * state
        out = [jnp.where(low, state, coef[:SUB, :]), jnp.where(low, before, coef[SUB:, :])]
        send_ref[pl.ds(start, 16), :] = jnp.concatenate(out, axis=0).astype(BF16)
        return (even_own + decay * odd_own) + squared * state, far + odd * state, far_even + even * before

    zero = jnp.zeros((SUB, LANES), F32)
    _, far, far_even = lax.fori_loop(0, blocks // 2, step, (zero, zero, zero), unroll=8)
    far = swap_quarters((far + far_even) * gains)
    me = lax.axis_index("ctx")
    mine = slab_rows(me // QUADS, blocks // QUADS)
    extra = [jnp.where(place == 4 + me % QUADS, wide(far[4 + q : 5 + q, :]), 0.0) for q in range(QUADS - 1, -1, -1)]
    send_ref[mine, :] = (send_ref[mine, :].astype(F32) + jnp.concatenate(extra, axis=0)).astype(BF16)


def total_kernel(received_ref, out_ref):
    def step(at, held):
        rows = received_ref[pl.ds(pl.multiple_of(at * 16, 16), 16), :].astype(F32)
        return held[0] + rows[:SUB, :], held[1] + rows[SUB:, :]

    zero = jnp.zeros((SUB, LANES), F32)
    first, second = lax.fori_loop(0, received_ref.shape[0] // 16, step, (zero, zero), unroll=8)
    total = first + second
    width = out_ref.shape[1]
    for k in range(QUADS):
        for j in range(4):
            out_ref[4 * k + j : 4 * k + j + 1, :] = total[4 + k : 5 + k, width * j : width * j + width]


def stage_kernel(
    mixed_far, rate_far, residue_far, lead_far, key_far, value_far, grad_far, conv_far,
    near_far, reach_far, power_far, gate_far, near_head, lead_head, reach_head, power_head, key_head, value_head,
    mixed_ref, rate_ref, residue_ref, near_ref, reach_ref, power_ref, grad_ref, conv_ref, gate_ref, weights, taps, sems,
):
    width = near_head.shape[1]
    steps = mixed_ref.shape[1] // width
    heads = ((lead_far, lead_head), (key_far, key_head), (value_far, value_head))
    pairs = [(rate_far, rate_ref), (residue_far, residue_ref), (mixed_far, mixed_ref), (grad_far, grad_ref), (conv_far, conv_ref)]
    pairs += [(far.at[:, pl.ds(0, width)], head) for far, head in heads]
    coming = [pltpu.make_async_copy(*pair, sems.at[i, 0]) for i, pair in enumerate(pairs)]
    for each in coming:
        each.start()
    for each in coming[:2]:
        each.wait()
    power_ref[...] = jnp.exp(-rate_ref[...])
    term = residue_ref[...] * gain_of(rate_ref[...])
    for d in range(ROWS):
        taps[d : d + 1, :] = jnp.sum(term, axis=0, keepdims=True)
        term = term * power_ref[...]
        if d == 0:
            weights[...] = term
    back = (16 * (SUB - 1 - lax.broadcasted_iota(jnp.int32, (SUB, LANES), 0))).astype(F32)
    for each in coming[2:5]:
        each.wait()

    def out_copy(i, at):
        source, target = ((near_ref, near_far), (reach_ref, reach_far), (power_ref, power_far), (gate_ref, gate_far))[i]
        lanes = pl.ds(pl.multiple_of(at * width, width), width)
        return pltpu.make_async_copy(source.at[:, lanes], target.at[:, lanes], sems.at[len(pairs) + i, at])

    def body(tile, slot):
        lanes = lane_slice(tile)
        gate_ref[:, lanes] = (grad_ref[:, lanes].astype(F32) * conv_ref[:, lanes].astype(F32)).astype(BF16)
        g = []
        for j in range(0, ROWS, 2):
            pair = mixed_ref[SUB * j : SUB * j + 16, lanes].astype(F32)
            g += [pair[:SUB, :], pair[SUB:, :]]
        near = [None] * ROWS
        for d in range(ROWS):
            tap = wide(taps[d : d + 1, lanes])
            for j in range(ROWS - d):
                near[j] = tap * g[j + d] if d == 0 else near[j] + tap * g[j + d]
        for j in range(ROWS):
            near_ref[SUB * j : SUB * j + SUB, lanes] = near[j]
        for m in range(MODES):
            reach = jnp.exp(-back * wide(rate_ref[m : m + 1, lanes]))
            reach_ref[SUB * m : SUB * m + SUB, lanes] = reach * wide(weights[m : m + 1, lanes])

    def step(at, _):
        each_tile(width, lambda tile, slot: body(tile + at * (width // LANES), slot))
        for i in range(4):
            out_copy(i, at).start()
        return 0

    lax.fori_loop(0, steps, step, 0)
    near_head[...] = near_ref[:, :width]
    reach_head[...] = reach_ref[:, :width]
    power_head[...] = power_ref[:, :width]
    for each in coming[5:]:
        each.wait()
    for at in range(steps):
        for i in range(4):
            out_copy(i, at).wait()


def output_kernel(
    near_ref, lead_ref, reach_ref, power_ref, key_ref, value_ref, received_ref,
    grad_key_ref, grad_value_ref,
    slabs, mixes,
):
    def body(tile, slot):
        lanes = lane_slice(tile)
        slab, mix_sub = slabs.at[slot], mixes.at[slot]
        slab[...] = received_ref[slab_rows(tile, near_ref.shape[1] // LANES), :].astype(F32)
        one = [wide(power_ref[m : m + 1, lanes]) for m in range(MODES)]
        state = []
        for m in range(MODES):
            row = SUB * (QUADS - 1 - m // 4) + m % 4
            rows = slice(SUB * m, SUB * m + SUB)
            state.append(lead_ref[rows, lanes] + wide(slab[row : row + 1, :]) * reach_ref[rows, lanes])
        for j in range(ROWS - 1, -1, -1):
            rows = slice(SUB * j, SUB * j + SUB)
            mix_sub[rows, :] = near_ref[rows, lanes] + halves_sum(state)
            if j > 0:
                state = [s * a for s, a in zip(state, one)]
        for i in range(0, ROWS, 2):
            rows = slice(SUB * i, SUB * i + 16)
            mix = jnp.concatenate([natural(mix_sub, i), natural(mix_sub, i + 1)], axis=0).astype(BF16).astype(F32)
            grad_key_ref[rows, lanes] = (mix * value_ref[rows, lanes].astype(F32)).astype(BF16)
            grad_value_ref[rows, lanes] = (mix * key_ref[rows, lanes].astype(F32)).astype(BF16)

    each_tile(near_ref.shape[1], body, 8)


def streamed(body, ins, outs, width, scratch, flops, moved, heads=(), ahead=3):
    arrays = [x for x, _ in ins + outs]
    n_in, n_all = len(ins), len(ins) + len(outs)
    stays = [kept for _, kept in ins + outs]
    steps = max(x.shape[1] for x in arrays) // width
    moving = [i for i in range(n_all) if not stays[i]]
    first = 1 if heads else 0

    def block(ref, at):
        if ref.shape[1] == LANES:
            size = width // LANES * 32
            return ref.at[pl.ds(pl.multiple_of((at ^ (FIRST * SUB // size)) * size, size), size), :]
        return ref.at[:, pl.ds(pl.multiple_of(at * width, width), width)]

    def kernel(*refs):
        ready = refs[n_in : n_in + len(heads)]
        refs = refs[:n_in] + refs[n_in + len(heads) :]
        places = dict(zip(moving, refs[n_all : n_all + len(moving)]))
        sems, *extra = refs[n_all + len(moving) :]

        def copy(i, at):
            ends = (block(refs[i], at), block(places[i], at))
            return pltpu.make_async_copy(*(ends if i < n_in else ends[::-1]), sems.at[i, at])

        coming = [i for i in moving if i < n_in]
        going = [i for i in moving if i >= n_in]
        for at in range(first, min(first + ahead, steps)):
            for i in coming:
                copy(i, at).start()

        def work(at, held):
            body(*(held.get(i, block(places.get(i, refs[i]), at)) for i in range(n_all)), *extra)
            for i in going:
                copy(i, at).start()

        def step(at, _):
            @pl.when(at + ahead < steps)
            def _():
                for i in coming:
                    copy(i, at + ahead).start()

            for i in coming:
                copy(i, at).wait()
            work(at, {})
            return 0

        if heads:
            work(0, dict(zip(coming, ready)))
        lax.fori_loop(first, steps, step, 0)
        for at in range(steps):
            for i in going:
                copy(i, at).wait()

    space = [pltpu.VMEM if kept else pltpu.HBM for kept in stays]
    specs = [pl.BlockSpec(memory_space=kind) for kind in space]
    held = [pltpu.with_memory_space_constraint(x, kind) for x, kind in zip(arrays[:n_in], space)]
    held += [pltpu.with_memory_space_constraint(x, pltpu.VMEM) for x in heads]
    results = [kind(x.shape, x.dtype) for x, kind in zip(arrays[n_in:], space[n_in:])]
    return call(
        kernel, (), specs[:n_in] + [pl.BlockSpec(memory_space=pltpu.VMEM)] * len(heads), specs[n_in:], results,
        [pltpu.VMEM(arrays[i].shape, arrays[i].dtype) for i in moving]
        + [pltpu.SemaphoreType.DMA((n_all, steps))]
        + scratch,
        flops, moved, STREAM_LIMIT,
    )(*held)


def call(kernel, grid, in_specs, out_specs, out_shape, scratch=(), flops=10**6, moved=2**20, limit=VMEM_LIMIT):
    return pl.pallas_call(
        kernel,
        grid=grid,
        in_specs=in_specs,
        out_specs=out_specs,
        out_shape=out_shape,
        scratch_shapes=scratch,
        compiler_params=pltpu.CompilerParams(vmem_limit_bytes=limit),
        cost_estimate=pl.CostEstimate(flops=flops, bytes_accessed=moved, transcendentals=0),
    )


def local(query_rows, key_rows, value_rows, conv_rows, grad_rows, residues, decay_rates):
    blocks = lax.axis_size("ctx")
    tokens, channels = query_rows.shape[1:]
    own = channels // blocks
    scale = 1.0 / math.sqrt(blocks * tokens)
    query, key, value, conv, grad = (x[0] for x in (query_rows, key_rows, value_rows, conv_rows, grad_rows))
    rates, residue = decay_rates.T, residues.T

    def table(*shape):
        return pltpu.VMEM(shape, F32)

    token_block = pl.BlockSpec((tokens, WIDTH), lambda n: (0, n))
    mode_block = pl.BlockSpec((MODES, WIDTH), lambda n: (0, n))
    slab_block = pl.BlockSpec((WIDTH // LANES * 32, LANES), lambda n: (n ^ (FIRST * SUB // (WIDTH // LANES * 32)), 0))
    token_half = jax.ShapeDtypeStruct((tokens, channels), BF16)
    token_full = jax.ShapeDtypeStruct((tokens, channels), F32)
    slabs = jax.ShapeDtypeStruct((blocks * SUB, LANES), BF16)
    steps = (channels // WIDTH,)

    mixed, product, states, entries, summary, rate_own = call(
        summary_kernel, steps,
        [token_block] * 4 + [mode_block],
        [token_block] * 4 + [slab_block, pl.BlockSpec((SUB, LANES), lambda n: (0, 0))],
        [token_half, token_half, token_full, token_full, slabs, jax.ShapeDtypeStruct((SUB, LANES), F32)],
        [table(4, MODES, WIDTH), table(2, 2, SUB * PITCH, LANES)],
        10**9, 10 * 2**20,
    )(grad, query, key, value, rates)

    def exchange(rows):
        pieces = rows.reshape(blocks, SUB, LANES)
        order = [[j ^ FIRST for j in range(blocks)]]
        moved = lax.all_to_all(pieces, "ctx", split_axis=0, concat_axis=0, axis_index_groups=order, tiled=True)
        return moved.reshape(blocks * SUB, LANES)

    received = exchange(summary)

    lead, coef_slabs = streamed(
        functools.partial(local_kernel, scale),
        [(x, False) for x in (mixed, product, states, entries, rates, residue)],
        [(token_full, False), (slabs, True)],
        WIDTH,
        [
            table(MODES, WIDTH), table(MODES, WIDTH), table(2, MODES, WIDTH),
            table(8, 32, LANES), table(3, MODES, WIDTH),
        ],
        10**9, 10 * 2**20,
    )

    vmem = pl.BlockSpec(memory_space=pltpu.VMEM)
    carries = call(
        functools.partial(scan_kernel, scale), (), [vmem] * 3, vmem, slabs, limit=SMALL_LIMIT
    )(received, coef_slabs, rate_own)

    returned = exchange(carries)

    conv_late, key_late, value_late, mixed_late, grad_late, _ = lax.optimization_barrier(
        (conv, key, value, mixed, grad, carries)
    )
    far_spec, near_spec = pl.BlockSpec(memory_space=pltpu.HBM), pl.BlockSpec(memory_space=pltpu.VMEM)
    head_types = [pltpu.VMEM((x.shape[0], WIDTH), x.dtype) for x in (lead, lead, lead, rates, key, value)]
    near, reach, power, grad_query, *heads = call(
        stage_kernel, (), [far_spec] * 8, [far_spec] * 4 + [near_spec] * 6,
        [pltpu.HBM(x.shape, x.dtype) for x in (lead, lead, rates, key)] + head_types,
        [pltpu.VMEM(mixed.shape, BF16)]
        + [pltpu.VMEM(x.shape, F32) for x in (rates, rates, lead, lead, rates)]
        + [pltpu.VMEM(mixed.shape, BF16)] * 3
        + [pltpu.VMEM(x.shape, F32) for x in (rates, rates)]
        + [pltpu.SemaphoreType.DMA((12, steps[0]))],
        10**9, 8 * 2**20, STREAM_LIMIT,
    )(*(
        pltpu.with_memory_space_constraint(x, pltpu.HBM)
        for x in (mixed_late, rates, residue, lead, key_late, value_late, grad_late, conv_late)
    ))

    coef_part = call(
        total_kernel, (), [vmem], vmem, jax.ShapeDtypeStruct((MODES, own), F32), limit=SMALL_LIMIT
    )(returned)
    other = lax.ppermute(coef_part, "dp", [(0, 1), (1, 0)])

    grad_key, grad_value = streamed(
        output_kernel,
        [(x, False) for x in (near, lead, reach, power, key, value)] + [(returned, True)],
        [(token_half, False), (token_half, False)],
        WIDTH,
        [table(8, 32, LANES), table(8, TOKENS, LANES)],
        10**9, 9 * 2**20, heads,
    )

    coef = (coef_part + other).T
    return (grad_query[None], grad_key[None], grad_value[None], coef)


def solution(mesh):
    rows = P("dp", "ctx", None)
    return jax.shard_map(
        local,
        mesh=mesh,
        in_specs=(rows, rows, rows, rows, rows, P(), P()),
        out_specs=(rows, rows, rows, P("ctx", None)),
        check_vma=False,
    )
```

```python
import functools
import math

import jax
import jax.numpy as jnp
from jax import lax
from jax.experimental import pallas as pl
from jax.experimental.pallas import tpu as pltpu
from jax.sharding import PartitionSpec as P

F32 = jnp.float32
BF16 = jnp.bfloat16
LANES = 128
SUB = 8
TOKENS = 128
ROWS = TOKENS // SUB
MODES = 16
QUADS = 4
PITCH = 24
FIRST = 107
WIDTH = 1024
VMEM_LIMIT = 60 * 1024 * 1024
SMALL_LIMIT = 4 * 1024 * 1024
STREAM_LIMIT = 40 * 1024 * 1024


def lane_slice(tile):
    return pl.ds(pl.multiple_of(tile * LANES, LANES), LANES)


def slab_rows(tile, tiles):
    return pl.ds(pl.multiple_of((tile ^ ((FIRST >> 2) & (tiles - 1))) * 32, 32), 32)


def gain_of(rates):
    square = rates * rates
    series = 1.0 + square * (1.0 / 6.0 + square * (1.0 / 120.0 + square * (1.0 / 5040.0)))
    return jnp.sqrt(2.0 * rates * series * jnp.exp(-rates))


def wide(row):
    return jnp.broadcast_to(row, (SUB, LANES))


def halves_sum(terms):
    while len(terms) > 1:
        terms = [x + y for x, y in zip(terms[::2], terms[1::2])]
    return terms[0]


def swap_quarters(tile):
    j = lax.broadcasted_iota(jnp.int32, (SUB, LANES), 0) & 3
    q = lax.broadcasted_iota(jnp.int32, (SUB, LANES), 1) >> 5
    for bit in (1, 2):
        j_set = (j & bit) != 0
        q_set = (q & bit) != 0
        up, down = pltpu.roll(tile, bit, 0), pltpu.roll(tile, SUB - bit, 0)
        if bit == 2:
            moved = pltpu.roll(jnp.where(j_set, up, down), 64, 1)
        else:
            moved = jnp.where(j_set, pltpu.roll(up, LANES - 32, 1), pltpu.roll(down, 32, 1))
        tile = jnp.where(j_set == q_set, tile, moved)
    return tile


def natural(tokens_sub, row):
    return tokens_sub[pl.ds(64 * (row % 2) + row // 2, SUB, stride=SUB), :]


def fold(first, second, bit, place):
    clear = (place & bit) == 0
    left = jnp.where(clear, first, pltpu.roll(second, bit, 0))
    right = jnp.where(clear, pltpu.roll(first, SUB - bit, 0), second)
    return left + right


def sublane_sums(tiles, place):
    for bit in (4, 2, 1):
        tiles = [fold(tiles[i], tiles[i + bit], bit, place) for i in range(bit)]
    return tiles[0]


def each_tile(width, body, slots=2):
    def some(at, _):
        for slot in range(slots):
            body(slots * at + slot, slot)
        return 0

    lax.fori_loop(0, width // (slots * LANES), some, 0)


def weighted_sums(state, entry, rows_of, place):
    for bit, power in ((4, 3), (2, 2), (1, 1)):
        clear = (place & bit) == 0
        weights = [rows_of(power, bit, i) for i in range(bit)]
        for which, tiles in enumerate((state, entry)):
            folded = []
            for i, weight in enumerate(weights):
                first, second = tiles[i], tiles[i + bit]
                left = jnp.where(clear, first, pltpu.roll(second, bit, 0))
                right = jnp.where(clear, pltpu.roll(first, SUB - bit, 0), second)
                folded.append(left + weight * right if which == 0 else right + weight * left)
            if which == 0:
                state = folded
            else:
                entry = folded
    return state[0], entry[0]


def summary_kernel(
    grad_ref, query_ref, key_ref, value_ref, rate_ref,
    mixed_ref, product_ref, state_ref, entry_ref, send_ref, own_ref,
    powers, full,
):
    rates = rate_ref[...]
    for index, power in enumerate((1.0, 16.0, 32.0, 64.0)):
        powers[index] = jnp.exp(-power * rates)
    place = lax.broadcasted_iota(jnp.int32, (SUB, LANES), 0)
    low = place < 4
    tiles = grad_ref.shape[1] // LANES
    me = lax.axis_index("ctx")
    tile_own, quad = me // QUADS, me % QUADS

    @pl.when(pl.program_id(0) == tile_own // tiles)
    def _():
        lanes = lane_slice(tile_own % tiles)
        eight = jnp.where(quad >= 2, rate_ref[SUB:, lanes], rate_ref[:SUB, lanes])
        turned = pltpu.roll(eight, 4, 0)
        own_ref[...] = jnp.where(low == (quad % 2 == 0), eight, turned)

    def body(tile, slot):
        lanes = lane_slice(tile)
        mixed_full, product_full = full.at[slot, 0], full.at[slot, 1]
        mixed = (grad_ref[:, lanes].astype(F32) * query_ref[:, lanes].astype(F32)).astype(BF16)
        product = (key_ref[:, lanes].astype(F32) * value_ref[:, lanes].astype(F32)).astype(BF16)
        mixed, product = mixed.astype(F32), product.astype(F32)
        for i in range(ROWS):
            at, rows = PITCH * (i // 2) + SUB * (i % 2), slice(SUB * i, SUB * i + SUB)
            mixed_full[at : at + SUB, :] = mixed[rows, :]
            product_full[at : at + SUB, :] = product[rows, :]
        g = [mixed_full[pl.ds(j, SUB, stride=PITCH), :] for j in range(ROWS)]
        p = [product_full[pl.ds(j, SUB, stride=PITCH), :] for j in range(ROWS)]
        for j in range(0, ROWS, 2):
            rows = slice(SUB * j, SUB * j + 16)
            mixed_ref[rows, lanes] = jnp.concatenate([g[j], g[j + 1]], axis=0).astype(BF16)
            product_ref[rows, lanes] = jnp.concatenate([p[j], p[j + 1]], axis=0).astype(BF16)
        sums = []
        for half in range(2):
            states, entries = [], []
            for base in range(SUB * half, SUB * half + SUB, 4):
                group = range(base, base + 4)
                one = [wide(powers[0, m : m + 1, lanes]) for m in group]
                state = [g[ROWS - 1]] * 4
                entry = [p[0] * a for a in one]
                for i in range(1, ROWS):
                    state = [s * a + g[ROWS - 1 - i] for s, a in zip(state, one)]
                    entry = [(e + p[i]) * a for e, a in zip(entry, one)]
                for s, e, m in zip(state, entry, group):
                    state_ref[SUB * m : SUB * m + SUB, lanes] = s
                    entry_ref[SUB * m : SUB * m + SUB, lanes] = e
                states += state
                entries += entry

            def rows_of(power, bit, i):
                if bit == 1:
                    return powers[power, SUB * half : SUB * half + SUB, lanes]
                modes = [SUB * half + i + bit * at for at in range(SUB // bit)]
                out = wide(powers[power, modes[-1] : modes[-1] + 1, lanes])
                for at in range(len(modes) - 2, -1, -1):
                    out = jnp.where(place < bit * (at + 1), wide(powers[power, modes[at] : modes[at] + 1, lanes]), out)
                return out

            s, e = weighted_sums(states, entries, rows_of, place)
            sums += [jnp.where(low, s, pltpu.roll(e, 4, 0)), jnp.where(low, pltpu.roll(s, 4, 0), e)]
        rows = slab_rows(tile, grad_ref.shape[1] // LANES)
        send_ref[rows, :] = jnp.concatenate(sums[::-1], axis=0).astype(BF16)

    each_tile(grad_ref.shape[1], body, 8)


def local_kernel(
    scale, mixed_ref, product_ref, state_ref, entry_ref, rate_ref, residue_ref,
    lead_ref, send_ref,
    powers, weights, lags, slabs, runs,
):
    rates = rate_ref[...]
    powers[...] = jnp.exp(-rates)
    gains = gain_of(rates)
    weights[...] = residue_ref[...] * gains * powers[...]
    for index, power in enumerate((16.0, 32.0, 64.0)):
        runs[index] = jnp.exp(-power * rates)
    place = lax.broadcasted_iota(jnp.int32, (SUB, LANES), 0)

    def body(tile, slot):
        lanes = lane_slice(tile)
        g, p = [], []
        for j in range(0, ROWS, 2):
            rows = slice(SUB * j, SUB * j + 16)
            pair = mixed_ref[rows, lanes].astype(F32)
            g += [pair[:SUB, :], pair[SUB:, :]]
            pair = product_ref[rows, lanes].astype(F32)
            p += [pair[:SUB, :], pair[SUB:, :]]
        lag = []
        for d in range(ROWS):
            total = g[d] * p[0]
            for j in range(1, ROWS - d):
                total = total + g[j + d] * p[j]
            lag.append(total)
        for half in range(2):
            rows = slice(SUB * half, SUB * half + SUB)
            lags[0, rows, lanes] = sublane_sums(lag[rows], place)
            cross = []
            for m in range(SUB * half, SUB * half + SUB):
                mode_rows = slice(SUB * m, SUB * m + SUB)
                carry = state_ref[mode_rows, lanes]
                for index, step in ((0, 1), (1, 2), (2, 4)):
                    later = jnp.where(place < SUB - step, pltpu.roll(carry, SUB - step, 0), 0.0)
                    carry = carry + wide(runs[index, m : m + 1, lanes]) * later
                carry = jnp.where(place < SUB - 1, pltpu.roll(carry, SUB - 1, 0), 0.0)
                cross.append(carry * entry_ref[mode_rows, lanes])
                lead_ref[mode_rows, lanes] = carry * wide(weights[m : m + 1, lanes])
            lags[1, rows, lanes] = sublane_sums(cross, place)

    each_tile(mixed_ref.shape[1], body, 4)
    coef = jnp.broadcast_to(lags[0, ROWS - 1 : ROWS, :], rates.shape)
    for d in range(ROWS - 2, -1, -1):
        coef = coef * powers[...] + lags[0, d : d + 1, :]
    lags[1] = (coef + lags[1]) * gains * scale
    slabs[...] = jnp.zeros_like(slabs)

    def ship(tile, slot):
        lanes = lane_slice(tile)
        slab = slabs.at[slot]
        for pair in range(2):
            moved = swap_quarters(lags[1, SUB * pair : SUB * pair + SUB, lanes])
            for k in range(2):
                for q in range(4):
                    row = SUB * (QUADS - 1 - q) + 4 + 2 * pair + k
                    slab[row : row + 1, :] = moved[4 * k + q : 4 * k + q + 1, :]
        send_ref[slab_rows(tile, mixed_ref.shape[1] // LANES), :] = slab[...].astype(BF16)

    each_tile(mixed_ref.shape[1], ship, 8)


def scan_kernel(scale, received_ref, coef_ref, rate_ref, send_ref):
    blocks = received_ref.shape[0] // SUB
    rates = rate_ref[...]
    decay = jnp.exp(-float(TOKENS) * rates)
    place = lax.broadcasted_iota(jnp.int32, (SUB, LANES), 0)
    low = place < 4

    squared = decay * decay
    gains = gain_of(rates) * scale

    def step(back, held):
        state, far, far_even = held
        start = pl.multiple_of(((blocks // 2 - 1 - back) ^ (FIRST >> 1)) * 16, 16)
        pair = received_ref[pl.ds(start, 16), :].astype(F32)
        coef = coef_ref[pl.ds(start, 16), :].astype(F32)
        odd, even = pair[:SUB, :], pair[SUB:, :]
        odd_own = jnp.where(low, odd, pltpu.roll(odd, 4, 0))
        even_own = jnp.where(low, even, pltpu.roll(even, 4, 0))
        before = odd_own + decay * state
        out = [jnp.where(low, state, coef[:SUB, :]), jnp.where(low, before, coef[SUB:, :])]
        send_ref[pl.ds(start, 16), :] = jnp.concatenate(out, axis=0).astype(BF16)
        return (even_own + decay * odd_own) + squared * state, far + odd * state, far_even + even * before

    zero = jnp.zeros((SUB, LANES), F32)
    _, far, far_even = lax.fori_loop(0, blocks // 2, step, (zero, zero, zero), unroll=8)
    far = swap_quarters((far + far_even) * gains)
    me = lax.axis_index("ctx")
    mine = slab_rows(me // QUADS, blocks // QUADS)
    extra = [jnp.where(place == 4 + me % QUADS, wide(far[4 + q : 5 + q, :]), 0.0) for q in range(QUADS - 1, -1, -1)]
    send_ref[mine, :] = (send_ref[mine, :].astype(F32) + jnp.concatenate(extra, axis=0)).astype(BF16)


def total_kernel(received_ref, out_ref):
    def step(at, held):
        rows = received_ref[pl.ds(pl.multiple_of(at * 16, 16), 16), :].astype(F32)
        return held[0] + rows[:SUB, :], held[1] + rows[SUB:, :]

    zero = jnp.zeros((SUB, LANES), F32)
    first, second = lax.fori_loop(0, received_ref.shape[0] // 16, step, (zero, zero), unroll=8)
    total = first + second
    width = out_ref.shape[1]
    for k in range(QUADS):
        for j in range(4):
            out_ref[4 * k + j : 4 * k + j + 1, :] = total[4 + k : 5 + k, width * j : width * j + width]


def stage_kernel(
    mixed_far, rate_far, residue_far, lead_far, key_far, value_far, grad_far, conv_far,
    near_far, reach_far, power_far, gate_far, near_head, lead_head, reach_head, power_head, key_head, value_head,
    mixed_ref, rate_ref, residue_ref, near_ref, reach_ref, power_ref, grad_ref, conv_ref, gate_ref, weights, taps, sems,
):
    width = near_head.shape[1]
    steps = mixed_ref.shape[1] // width
    heads = ((lead_far, lead_head), (key_far, key_head), (value_far, value_head))
    pairs = [(rate_far, rate_ref), (residue_far, residue_ref), (mixed_far, mixed_ref), (grad_far, grad_ref), (conv_far, conv_ref)]
    pairs += [(far.at[:, pl.ds(0, width)], head) for far, head in heads]
    coming = [pltpu.make_async_copy(*pair, sems.at[i, 0]) for i, pair in enumerate(pairs)]
    for each in coming:
        each.start()
    for each in coming[:2]:
        each.wait()
    power_ref[...] = jnp.exp(-rate_ref[...])
    term = residue_ref[...] * gain_of(rate_ref[...])
    for d in range(ROWS):
        taps[d : d + 1, :] = jnp.sum(term, axis=0, keepdims=True)
        term = term * power_ref[...]
        if d == 0:
            weights[...] = term
    back = (16 * (SUB - 1 - lax.broadcasted_iota(jnp.int32, (SUB, LANES), 0))).astype(F32)
    for each in coming[2:5]:
        each.wait()

    def out_copy(i, at):
        source, target = ((near_ref, near_far), (reach_ref, reach_far), (power_ref, power_far), (gate_ref, gate_far))[i]
        lanes = pl.ds(pl.multiple_of(at * width, width), width)
        return pltpu.make_async_copy(source.at[:, lanes], target.at[:, lanes], sems.at[len(pairs) + i, at])

    def body(tile, slot):
        lanes = lane_slice(tile)
        gate_ref[:, lanes] = (grad_ref[:, lanes].astype(F32) * conv_ref[:, lanes].astype(F32)).astype(BF16)
        g = []
        for j in range(0, ROWS, 2):
            pair = mixed_ref[SUB * j : SUB * j + 16, lanes].astype(F32)
            g += [pair[:SUB, :], pair[SUB:, :]]
        near = [None] * ROWS
        for d in range(ROWS):
            tap = wide(taps[d : d + 1, lanes])
            for j in range(ROWS - d):
                near[j] = tap * g[j + d] if d == 0 else near[j] + tap * g[j + d]
        for j in range(ROWS):
            near_ref[SUB * j : SUB * j + SUB, lanes] = near[j]
        for m in range(MODES):
            reach = jnp.exp(-back * wide(rate_ref[m : m + 1, lanes]))
            reach_ref[SUB * m : SUB * m + SUB, lanes] = reach * wide(weights[m : m + 1, lanes])

    def step(at, _):
        each_tile(width, lambda tile, slot: body(tile + at * (width // LANES), slot))
        for i in range(4):
            out_copy(i, at).start()
        return 0

    lax.fori_loop(0, steps, step, 0)
    near_head[...] = near_ref[:, :width]
    reach_head[...] = reach_ref[:, :width]
    power_head[...] = power_ref[:, :width]
    for each in coming[5:]:
        each.wait()
    for at in range(steps):
        for i in range(4):
            out_copy(i, at).wait()


def output_kernel(
    near_ref, lead_ref, reach_ref, power_ref, key_ref, value_ref, received_ref,
    grad_key_ref, grad_value_ref,
    slabs, mixes,
):
    def body(tile, slot):
        lanes = lane_slice(tile)
        slab, mix_sub = slabs.at[slot], mixes.at[slot]
        slab[...] = received_ref[slab_rows(tile, near_ref.shape[1] // LANES), :].astype(F32)
        one = [wide(power_ref[m : m + 1, lanes]) for m in range(MODES)]
        state = []
        for m in range(MODES):
            row = SUB * (QUADS - 1 - m // 4) + m % 4
            rows = slice(SUB * m, SUB * m + SUB)
            state.append(lead_ref[rows, lanes] + wide(slab[row : row + 1, :]) * reach_ref[rows, lanes])
        for j in range(ROWS - 1, -1, -1):
            rows = slice(SUB * j, SUB * j + SUB)
            mix_sub[rows, :] = near_ref[rows, lanes] + halves_sum(state)
            if j > 0:
                state = [s * a for s, a in zip(state, one)]
        for i in range(0, ROWS, 2):
            rows = slice(SUB * i, SUB * i + 16)
            mix = jnp.concatenate([natural(mix_sub, i), natural(mix_sub, i + 1)], axis=0).astype(BF16).astype(F32)
            grad_key_ref[rows, lanes] = (mix * value_ref[rows, lanes].astype(F32)).astype(BF16)
            grad_value_ref[rows, lanes] = (mix * key_ref[rows, lanes].astype(F32)).astype(BF16)

    each_tile(near_ref.shape[1], body, 8)


def streamed(body, ins, outs, width, scratch, flops, moved, heads=(), ahead=3):
    arrays = [x for x, _ in ins + outs]
    n_in, n_all = len(ins), len(ins) + len(outs)
    stays = [kept for _, kept in ins + outs]
    steps = max(x.shape[1] for x in arrays) // width
    moving = [i for i in range(n_all) if not stays[i]]
    first = 1 if heads else 0

    def block(ref, at):
        if ref.shape[1] == LANES:
            size = width // LANES * 32
            return ref.at[pl.ds(pl.multiple_of((at ^ (FIRST * SUB // size)) * size, size), size), :]
        return ref.at[:, pl.ds(pl.multiple_of(at * width, width), width)]

    def kernel(*refs):
        ready = refs[n_in : n_in + len(heads)]
        refs = refs[:n_in] + refs[n_in + len(heads) :]
        places = dict(zip(moving, refs[n_all : n_all + len(moving)]))
        sems, *extra = refs[n_all + len(moving) :]

        def copy(i, at):
            ends = (block(refs[i], at), block(places[i], at))
            return pltpu.make_async_copy(*(ends if i < n_in else ends[::-1]), sems.at[i, at])

        coming = [i for i in moving if i < n_in]
        going = [i for i in moving if i >= n_in]
        for at in range(first, min(first + ahead, steps)):
            for i in coming:
                copy(i, at).start()

        def work(at, held):
            body(*(held.get(i, block(places.get(i, refs[i]), at)) for i in range(n_all)), *extra)
            for i in going:
                copy(i, at).start()

        def step(at, _):
            @pl.when(at + ahead < steps)
            def _():
                for i in coming:
                    copy(i, at + ahead).start()

            for i in coming:
                copy(i, at).wait()
            work(at, {})
            return 0

        if heads:
            work(0, dict(zip(coming, ready)))
        lax.fori_loop(first, steps, step, 0)
        for at in range(steps):
            for i in going:
                copy(i, at).wait()

    space = [pltpu.VMEM if kept else pltpu.HBM for kept in stays]
    specs = [pl.BlockSpec(memory_space=kind) for kind in space]
    held = [pltpu.with_memory_space_constraint(x, kind) for x, kind in zip(arrays[:n_in], space)]
    held += [pltpu.with_memory_space_constraint(x, pltpu.VMEM) for x in heads]
    results = [kind(x.shape, x.dtype) for x, kind in zip(arrays[n_in:], space[n_in:])]
    return call(
        kernel, (), specs[:n_in] + [pl.BlockSpec(memory_space=pltpu.VMEM)] * len(heads), specs[n_in:], results,
        [pltpu.VMEM(arrays[i].shape, arrays[i].dtype) for i in moving]
        + [pltpu.SemaphoreType.DMA((n_all, steps))]
        + scratch,
        flops, moved, STREAM_LIMIT,
    )(*held)


def call(kernel, grid, in_specs, out_specs, out_shape, scratch=(), flops=10**6, moved=2**20, limit=VMEM_LIMIT):
    return pl.pallas_call(
        kernel,
        grid=grid,
        in_specs=in_specs,
        out_specs=out_specs,
        out_shape=out_shape,
        scratch_shapes=scratch,
        compiler_params=pltpu.CompilerParams(vmem_limit_bytes=limit),
        cost_estimate=pl.CostEstimate(flops=flops, bytes_accessed=moved, transcendentals=0),
    )


def local(query_rows, key_rows, value_rows, conv_rows, grad_rows, residues, decay_rates):
    blocks = lax.axis_size("ctx")
    tokens, channels = query_rows.shape[1:]
    own = channels // blocks
    scale = 1.0 / math.sqrt(blocks * tokens)
    query, key, value, conv, grad = (x[0] for x in (query_rows, key_rows, value_rows, conv_rows, grad_rows))
    rates, residue = decay_rates.T, residues.T

    def table(*shape):
        return pltpu.VMEM(shape, F32)

    token_block = pl.BlockSpec((tokens, WIDTH), lambda n: (0, n))
    mode_block = pl.BlockSpec((MODES, WIDTH), lambda n: (0, n))
    slab_block = pl.BlockSpec((WIDTH // LANES * 32, LANES), lambda n: (n ^ (FIRST * SUB // (WIDTH // LANES * 32)), 0))
    token_half = jax.ShapeDtypeStruct((tokens, channels), BF16)
    token_full = jax.ShapeDtypeStruct((tokens, channels), F32)
    slabs = jax.ShapeDtypeStruct((blocks * SUB, LANES), BF16)
    steps = (channels // WIDTH,)

    mixed, product, states, entries, summary, rate_own = call(
        summary_kernel, steps,
        [token_block] * 4 + [mode_block],
        [token_block] * 4 + [slab_block, pl.BlockSpec((SUB, LANES), lambda n: (0, 0))],
        [token_half, token_half, token_full, token_full, slabs, jax.ShapeDtypeStruct((SUB, LANES), F32)],
        [table(4, MODES, WIDTH), table(8, 2, SUB * PITCH, LANES)],
        10**9, 10 * 2**20,
    )(grad, query, key, value, rates)

    def exchange(rows):
        pieces = rows.reshape(blocks, SUB, LANES)
        order = [[j ^ FIRST for j in range(blocks)]]
        moved = lax.all_to_all(pieces, "ctx", split_axis=0, concat_axis=0, axis_index_groups=order, tiled=True)
        return moved.reshape(blocks * SUB, LANES)

    received = exchange(summary)

    lead, coef_slabs = streamed(
        functools.partial(local_kernel, scale),
        [(x, False) for x in (mixed, product, states, entries, rates, residue)],
        [(token_full, False), (slabs, True)],
        WIDTH,
        [
            table(MODES, WIDTH), table(MODES, WIDTH), table(2, MODES, WIDTH),
            table(8, 32, LANES), table(3, MODES, WIDTH),
        ],
        10**9, 10 * 2**20,
    )

    vmem = pl.BlockSpec(memory_space=pltpu.VMEM)
    carries = call(
        functools.partial(scan_kernel, scale), (), [vmem] * 3, vmem, slabs, limit=SMALL_LIMIT
    )(received, coef_slabs, rate_own)

    returned = exchange(carries)

    conv_late, key_late, value_late, mixed_late, grad_late, _ = lax.optimization_barrier(
        (conv, key, value, mixed, grad, carries)
    )
    far_spec, near_spec = pl.BlockSpec(memory_space=pltpu.HBM), pl.BlockSpec(memory_space=pltpu.VMEM)
    head_types = [pltpu.VMEM((x.shape[0], WIDTH), x.dtype) for x in (lead, lead, lead, rates, key, value)]
    near, reach, power, grad_query, *heads = call(
        stage_kernel, (), [far_spec] * 8, [far_spec] * 4 + [near_spec] * 6,
        [pltpu.HBM(x.shape, x.dtype) for x in (lead, lead, rates, key)] + head_types,
        [pltpu.VMEM(mixed.shape, BF16)]
        + [pltpu.VMEM(x.shape, F32) for x in (rates, rates, lead, lead, rates)]
        + [pltpu.VMEM(mixed.shape, BF16)] * 3
        + [pltpu.VMEM(x.shape, F32) for x in (rates, rates)]
        + [pltpu.SemaphoreType.DMA((12, steps[0]))],
        10**9, 8 * 2**20, STREAM_LIMIT,
    )(*(
        pltpu.with_memory_space_constraint(x, pltpu.HBM)
        for x in (mixed_late, rates, residue, lead, key_late, value_late, grad_late, conv_late)
    ))

    coef_part = call(
        total_kernel, (), [vmem], vmem, jax.ShapeDtypeStruct((MODES, own), F32), limit=SMALL_LIMIT
    )(returned)
    other = lax.ppermute(coef_part, "dp", [(0, 1), (1, 0)])

    grad_key, grad_value = streamed(
        output_kernel,
        [(x, False) for x in (near, lead, reach, power, key, value)] + [(returned, True)],
        [(token_half, False), (token_half, False)],
        WIDTH,
        [table(8, 32, LANES), table(8, TOKENS, LANES)],
        10**9, 9 * 2**20, heads,
    )

    coef = (coef_part + other).T
    return (grad_query[None], grad_key[None], grad_value[None], coef)


def solution(mesh):
    rows = P("dp", "ctx", None)
    return jax.shard_map(
        local,
        mesh=mesh,
        in_specs=(rows, rows, rows, rows, rows, P(), P()),
        out_specs=(rows, rows, rows, P("ctx", None)),
        check_vma=False,
    )
```
